32 devices in a mesh: grp: 2 (over y), blk: 16 (over z, x, core).
Axes of the slice: x: 2, y: 2, z: 4, core: 2. Of those that a mesh axis runs over, the one named last changes fastest.
Arguments:
- images: bfloat16 [1024, 1152], P(('blk', 'grp')), may hold values from -6 to 6
- texts: bfloat16 [1024, 1152], P(('blk', 'grp')), may hold values from -6 to 6
- tile_mask: int32 [8, 8], replicated, may hold values from 0 to 1, as said below
Outputs:
- image_grads: float32 [1024, 1152], P(('blk', 'grp'))
- text_grads: float32 [1024, 1152], P(('blk', 'grp'))
- loss_mean: float32 [], replicated
The draws below stay inside these ranges and needn't reach their ends.
Inputs may be any that keep to these rules, and one draw needn't show every extreme that they name: tile_mask is symmetric and 1 on its diagonal.
All inputs are finite; a program needn't handle non-finite values.
Results may differ from the reference program's by a relative error of at most 0.00045.
The reference program's roundings to bfloat16 on the way (of `coef`) count: a program that leaves them out, or rounds other values in their place, can miss the bound.
Values may be sent and summed in bfloat16 or wider, within the bound.
A program may use at most 64 MiB of HBM per device.

```python
import math
import jax
import jax.numpy as jnp
from jax import lax

E = 1152
TILE = 128
TOTAL = 1024
TILES = 8


def draw_tile_mask(key, part):
    rows = jnp.arange(TILES, dtype=jnp.int32)[:, None]
    cols = jnp.arange(TILES, dtype=jnp.int32)[None, :]
    level = jax.random.randint(key, (TILES, TILES), 0, 4 * TILES)
    upper = (level >= rows + cols + TILES // 4).astype(jnp.int32)
    lower_index = jnp.minimum(rows, cols)
    upper_index = jnp.maximum(rows, cols)
    mirrored = upper[lower_index, upper_index]
    return jnp.where(rows == cols, 1, mirrored).astype(jnp.int32)


def shard_levels(own_key, extent, pieces, least, high):
    gain, own = 1.0, jax.random.fold_in(own_key, 6)
    for dim, parts in pieces:
        draws = jnp.exp(jax.random.uniform(jax.random.fold_in(own, dim), (parts,), jnp.float32, least / len(pieces), high / len(pieces)))
        gain = gain * jnp.repeat(draws, extent[dim] // parts).reshape([-1 if axis == dim else 1 for axis in range(len(extent))])
    return gain


def normal_values(key, dims, scale, reach, cuts=(), held_as=jnp.bfloat16):
    values = jax.random.normal(key, dims, jnp.float32) * scale
    if len(cuts) > 0:
        values = shard_levels(key, dims, cuts, -0.22, 0.18) * values
    return jnp.clip(values, min=-reach, max=reach).astype(held_as)


def setup_inputs(seed: int = 0) -> dict:
    keys = jax.random.split(jax.random.key(seed), 4)
    images = normal_values(keys[0], (TOTAL, E), 1.0, 6.0, ((0, 32),))
    texts = normal_values(keys[1], (TOTAL, E), 1.0, 6.0, ((0, 32),))
    tile_mask = draw_tile_mask(jax.random.fold_in(keys[3], 71), 0)
    return dict(images=images, texts=texts, tile_mask=tile_mask)


TEMP = 10.0
BIAS = -2.0
EPS = 1e-06

def normalize(values):
    return values * lax.rsqrt(lax.optimization_barrier(jnp.sum(values * values, axis=-1, keepdims=True)) + EPS)

def reference(images, texts, tile_mask):
    image_unit, image_back = jax.vjp(normalize, images.astype(jnp.float32))
    text_unit, text_back = jax.vjp(normalize, texts.astype(jnp.float32))
    image_bf = image_unit.astype(jnp.bfloat16)
    text_bf = text_unit.astype(jnp.bfloat16)
    all_ids = jnp.arange(TOTAL, dtype=jnp.int32)
    tile_ids = jnp.arange(TILES, dtype=jnp.int32)
    text_hot = (tile_ids[:, None] == (all_ids // TILE)[None, :]).astype(jnp.float32)
    mask_values = tile_mask.astype(jnp.float32)
    block = math.gcd(TOTAL, 512)
    starts = jnp.arange(TOTAL // block, dtype=jnp.int32) * block

    def step(carry, start):
        text_sums, loss_sum, pair_count = carry
        ids = start + jnp.arange(block, dtype=jnp.int32)
        hot = ((ids // TILE)[:, None] == tile_ids[None, :]).astype(jnp.float32)
        masked = jnp.dot(jnp.dot(hot, mask_values, precision=lax.Precision.HIGHEST), text_hot, precision=lax.Precision.HIGHEST)
        matched = ids[:, None] == all_ids[None, :]
        valid = (masked < 0.5) | matched
        rows_bf = lax.dynamic_slice_in_dim(image_bf, start, block, 0)
        logits = TEMP * jnp.dot(rows_bf, text_bf.T, preferred_element_type=jnp.float32) + BIAS
        signs = jnp.where(matched, 1.0, -1.0)
        loss_sum = loss_sum + jnp.sum(jnp.where(valid, jax.nn.softplus(-signs * logits), 0.0))
        pair_count = pair_count + jnp.sum(valid.astype(jnp.float32))
        coef = jnp.where(valid, jax.nn.sigmoid(logits) - matched.astype(jnp.float32), 0.0).astype(jnp.bfloat16)
        image_part = TEMP * jnp.dot(coef, text_bf, preferred_element_type=jnp.float32)
        text_sums = text_sums + jnp.dot(coef.T, rows_bf, preferred_element_type=jnp.float32)
        return ((text_sums, loss_sum, pair_count), image_part)
    initial = (jnp.zeros((TOTAL, E), jnp.float32), jnp.zeros((), jnp.float32), jnp.zeros((), jnp.float32))
    (text_sums, loss_sum, pair_count), image_parts = lax.scan(step, initial, starts)
    image_sums = image_parts.reshape(TOTAL, E)
    image_grads = image_back(image_sums)[0]
    text_grads = text_back(TEMP * text_sums)[0]
    return (image_grads, text_grads, loss_sum / pair_count)
```

```python
import functools

import jax
import jax.numpy as jnp
from jax import lax
from jax.experimental import pallas as pl
from jax.experimental.pallas import tpu as pltpu
from jax.sharding import PartitionSpec as P

TILE = 128
TEMP = 10.0
BIAS = -2.0
EPS = 1e-06
MESH = pl.DeviceIdType.MESH


def split_of(groups, loops, rows):
    best = None
    for inner in range(1, loops + 1):
        if loops % inner or (groups * inner * rows) % TILE:
            continue
        cost = groups * inner + loops // inner
        if best is None or cost <= best[0]:
            best = (cost, inner)
    return best[1]


def inverse_norm(x):
    return lax.rsqrt(jnp.sum(x * x, axis=-1, keepdims=True) + EPS)


def backward(x, g):
    r = inverse_norm(x)
    u = x * r
    return r * (g - u * jnp.sum(u * g, axis=-1, keepdims=True))


def each(count, body):
    if count == 1:
        body(0)
    else:
        lax.fori_loop(0, count, lambda i, c: (body(i), c)[1], 0)


def kernel(groups, loops, inner, mask_s, mask_v, img_ref, txt_ref,
           img_out, txt_out, loss_out,
           imgs, txts, coef, img_part, txt_part, img_in, txt_in, loss_a, loss_b,
           img_send, img_recv, txt_send, txt_recv,
           ip_send, ip_recv, tp_send, tp_recv,
           la_send, la_recv, lb_send, lb_recv):
    rows = img_ref.shape[0]
    across = groups * inner
    along = loops // inner
    g = lax.axis_index("grp")
    b = lax.axis_index("blk")
    o, i = b // inner, b % inner
    m = i * groups + g
    wide, tall = across * rows, along * rows

    def image_peer(d):
        p = lax.rem(m + d, across)
        return p, {"grp": p % groups, "blk": o * inner + p // groups}

    def text_peer(d):
        p = lax.rem(o + d, along)
        return p, {"grp": g, "blk": p * inner + i}

    def block(ref, p):
        return ref.at[pl.ds(pl.multiple_of(p * rows, rows), rows)]

    def copy(src, dst, send, recv, to):
        return pltpu.make_async_remote_copy(
            src_ref=src, dst_ref=dst, send_sem=send, recv_sem=recv,
            device_id=to, device_id_type=MESH)

    def image_copy(d, arriving=False):
        p, to = image_peer(d)
        at = p if arriving else m
        return copy(block(imgs, at), block(imgs, at), img_send.at[d], img_recv.at[at], to)

    def text_copy(d, arriving=False):
        p, to = text_peer(d)
        at = p if arriving else o
        return copy(block(txts, at), block(txts, at), txt_send.at[d], txt_recv.at[at], to)

    def image_sum_copy(d, arriving=False):
        p, to = image_peer(d)
        at = p if arriving else m
        return copy(block(img_part, p), img_in.at[at], ip_send.at[d], ip_recv.at[at], to)

    def text_sum_copy(d, arriving=False):
        p, to = text_peer(d)
        at = p if arriving else o
        return copy(block(txt_part, p), txt_in.at[at], tp_send.at[d], tp_recv.at[at], to)

    def loss_a_copy(d, arriving=False):
        p, to = image_peer(d)
        at = p if arriving else m
        return copy(loss_a.at[m], loss_a.at[at], la_send.at[d], la_recv.at[at], to)

    def loss_b_copy(d, arriving=False):
        p, to = text_peer(d)
        at = p if arriving else o
        return copy(loss_b.at[o], loss_b.at[at], lb_send.at[d], lb_recv.at[at], to)

    barrier = pltpu.get_barrier_semaphore()
    for d in range(1, along):
        pl.semaphore_signal(barrier, inc=1, device_id=text_peer(d)[1], device_id_type=MESH)
    for d in range(1, across):
        pl.semaphore_signal(barrier, inc=1, device_id=image_peer(d)[1], device_id_type=MESH)

    x = txt_ref[...].astype(jnp.float32)
    block(txts, o)[...] = (x * inverse_norm(x)).astype(jnp.bfloat16)
    x = img_ref[...].astype(jnp.float32)
    block(imgs, m)[...] = (x * inverse_norm(x)).astype(jnp.bfloat16)
    pl.semaphore_wait(barrier, along + across - 2)

    for d in range(1, along):
        text_copy(d).start()
    for d in range(1, across):
        image_copy(d).start()
    loss_a[m] = jnp.zeros_like(loss_a[m])
    for d in range(1, across):
        image_copy(d, True).wait_recv()
    for d in range(1, along):
        text_copy(d, True).wait_recv()

    tb, ib = min(tall, 128), min(wide, 256)
    pieces = tb // rows

    def terms(step):
        t, n = step // (wide // ib), step % (wide // ib)
        t_at, n_at = pl.multiple_of(t * tb, tb), pl.multiple_of(n * ib, ib)
        logits = TEMP * lax.dot_general(
            txts[pl.ds(t_at, tb)], imgs[pl.ds(n_at, ib)],
            (((1,), (1,)), ((), ())), preferred_element_type=jnp.float32) + BIAS
        held, ids = [], []
        iota = lax.broadcasted_iota(jnp.int32, (rows, TILE), 0)
        for k in range(pieces):
            start = (((t * pieces + k) * inner + i) * groups + g) * rows
            held.append(jnp.concatenate([
                jnp.full((rows, TILE), mask_s[start // TILE, (o * wide + n_at) // TILE + j], jnp.int32)
                for j in range(ib // TILE)], axis=1))
            ids.append(jnp.concatenate([start + iota] * (ib // TILE), axis=1))
        held, text_ids = jnp.concatenate(held, axis=0), jnp.concatenate(ids, axis=0)
        image_ids = o * wide + n_at + lax.broadcasted_iota(jnp.int32, (tb, ib), 1)
        matched = text_ids == image_ids
        valid = (held == 0) | matched
        z = jnp.where(matched, -logits, logits)
        e = jnp.exp(-jnp.abs(logits))
        loss = jnp.where(valid, jnp.maximum(z, 0.0) + jnp.log1p(e), 0.0)
        sig = jnp.where(logits >= 0, 1.0, e) / (1.0 + e)
        value = jnp.where(valid, sig - matched.astype(jnp.float32), 0.0)
        coef[pl.ds(t_at, tb), pl.ds(n_at, ib)] = value.astype(jnp.bfloat16)
        loss = sum(loss[:, j * TILE:(j + 1) * TILE] for j in range(ib // TILE))
        loss_a[m] += jnp.sum(loss.reshape(tb // 8, 8, TILE), axis=0)

    each((tall // tb) * (wide // ib), terms)
    for d in range(1, across):
        loss_a_copy(d).start()

    def text_sums(t):
        t_at = pl.multiple_of(t * tb, tb)
        txt_part[pl.ds(t_at, tb)] = jnp.dot(
            coef[pl.ds(t_at, tb)], imgs[...], preferred_element_type=jnp.float32)

    each(tall // tb, text_sums)
    for d in range(1, along):
        text_sum_copy(d).start()

    def image_sums(n):
        n_at = pl.multiple_of(n * ib, ib)
        img_part[pl.ds(n_at, ib)] = lax.dot_general(
            coef[:, pl.ds(n_at, ib)], txts[...], (((0,), (0,)), ((), ())),
            preferred_element_type=jnp.float32)

    each(wide // ib, image_sums)
    for d in range(1, across):
        image_sum_copy(d).start()

    for d in range(1, across):
        loss_a_copy(d, True).wait_recv()
    loss_b[o] = jnp.sum(loss_a[...], axis=0)
    for d in range(1, along):
        loss_b_copy(d).start()

    total = block(img_part, m)[...]
    for d in range(1, across):
        image_sum_copy(d, True).wait_recv()
        total += img_in[image_peer(d)[0]]
    img_out[...] = backward(img_ref[...].astype(jnp.float32), TEMP * total)

    for d in range(1, along):
        loss_b_copy(d, True).wait_recv()
    loss = jnp.sum(jnp.sum(loss_b[...], axis=0), keepdims=True)
    open_tiles = jnp.sum((mask_v[...] == 0).astype(jnp.float32), keepdims=True)
    loss_out[...] = loss / (open_tiles * (TILE * TILE) + (loops * groups * rows))

    total = block(txt_part, o)[...]
    for d in range(1, along):
        text_sum_copy(d, True).wait_recv()
        total += txt_in[text_peer(d)[0]]
    txt_out[...] = backward(txt_ref[...].astype(jnp.float32), TEMP * total)

    for d in range(1, across):
        image_copy(d).wait_send()
        image_sum_copy(d).wait_send()
        loss_a_copy(d).wait_send()
    for d in range(1, along):
        text_copy(d).wait_send()
        text_sum_copy(d).wait_send()
        loss_b_copy(d).wait_send()


def solution(mesh):
    groups, loops = mesh.shape["grp"], mesh.shape["blk"]

    def on_device(images, texts, tile_mask):
        rows, width = images.shape
        inner = split_of(groups, loops, rows)
        across, along = groups * inner, loops // inner
        wide, tall = across * rows, along * rows
        dma = pltpu.SemaphoreType.DMA
        vmem = pl.BlockSpec(memory_space=pltpu.VMEM)
        image_grads, text_grads, loss = pl.pallas_call(
            functools.partial(kernel, groups, loops, inner),
            out_shape=(
                jax.ShapeDtypeStruct((rows, width), jnp.float32),
                jax.ShapeDtypeStruct((rows, width), jnp.float32),
                jax.ShapeDtypeStruct((1, 1), jnp.float32),
            ),
            in_specs=[pl.BlockSpec(memory_space=pltpu.SMEM), vmem, vmem, vmem],
            out_specs=(vmem, vmem, vmem),
            scratch_shapes=[
                pltpu.VMEM((wide, width), jnp.bfloat16),
                pltpu.VMEM((tall, width), jnp.bfloat16),
                pltpu.VMEM((tall, wide), jnp.bfloat16),
                pltpu.VMEM((wide, width), jnp.float32),
                pltpu.VMEM((tall, width), jnp.float32),
                pltpu.VMEM((across, rows, width), jnp.float32),
                pltpu.VMEM((along, rows, width), jnp.float32),
                pltpu.VMEM((across, 8, TILE), jnp.float32),
                pltpu.VMEM((along, 8, TILE), jnp.float32),
            ] + [dma((across,)), dma((across,)), dma((along,)), dma((along,))] * 3,
            compiler_params=pltpu.CompilerParams(
                collective_id=0, has_side_effects=True, vmem_limit_bytes=40 * 2**20),
        )(tile_mask, tile_mask, images, texts)
        return image_grads, text_grads, loss[0, 0]

    return jax.shard_map(
        on_device,
        mesh=mesh,
        in_specs=(P(("blk", "grp"), None), P(("blk", "grp"), None), P()),
        out_specs=(P(("blk", "grp"), None), P(("blk", "grp"), None), P()),
        check_vma=False,
    )
```

```python
import functools

import jax
import jax.numpy as jnp
from jax import lax
from jax.experimental import pallas as pl
from jax.experimental.pallas import tpu as pltpu
from jax.sharding import PartitionSpec as P

TILE = 128
TEMP = 10.0
BIAS = -2.0
EPS = 1e-06
LOG_2 = 0.6931471805599453
MESH = pl.DeviceIdType.MESH


def split_of(groups, loops, rows):
    best = None
    for inner in range(1, loops + 1):
        if loops % inner or (groups * inner * rows) % TILE:
            continue
        cost = groups * inner + loops // inner
        if best is None or cost <= best[0]:
            best = (cost, inner)
    return best[1]


def inverse_norm(x):
    return lax.rsqrt(jnp.sum(x * x, axis=-1, keepdims=True) + EPS)


def backward(x, g):
    r = inverse_norm(x)
    u = x * r
    return r * (g - u * jnp.sum(u * g, axis=-1, keepdims=True))


def flipped(place, bits):
    bit = 1
    while bit <= bits:
        if bits & bit:
            place = place + bit - 2 * bit * ((place // bit) % 2)
        bit *= 2
    return place


def step_of(exponent):
    return jnp.exp((exponent - 15.0) * LOG_2)


def pack(value):
    half = value.shape[0] // 2
    most = jnp.max(jnp.abs(value), axis=-1, keepdims=True)
    exponent = jnp.floor(jnp.log(jnp.maximum(most, 1e-30)) * (1.0 / LOG_2)) + 1.0
    fixed = jnp.clip(jnp.round(value * (1.0 / step_of(exponent))), -32767.0, 32767.0)
    fixed = jnp.concatenate(
        [fixed, jnp.broadcast_to(exponent, (value.shape[0], 128))], axis=1).astype(jnp.int32)
    return fixed[:half] * 65536 + (fixed[half:] & 65535)


def unpack(words):
    low = lax.shift_right_arithmetic(lax.shift_left(words, 16), 16)
    fixed = jnp.concatenate([lax.shift_right_arithmetic(words, 16), low], axis=0).astype(jnp.float32)
    width = fixed.shape[1] - 128
    return fixed[:, :width] * step_of(fixed[:, width:width + 1])


def kernel(groups, loops, inner, mask_hbm, img_hbm, txt_hbm,
           img_out, txt_out, loss_out,
           mask_s, mask_v, img_ref, txt_ref,
           imgs, txts, coef, img_part, txt_part, img_go, txt_go, img_in, txt_in, loss_a, loss_b,
           load_sem,
           img_send, img_recv, txt_send, txt_recv,
           ip_send, ip_recv, tp_send, tp_recv,
           la_send, la_recv, lb_send, lb_recv):
    rows = img_ref.shape[0]
    across = groups * inner
    along = loops // inner
    g = lax.axis_index("grp")
    b = lax.axis_index("blk")
    o, i = b // inner, b % inner
    m = i * groups + g
    wide, tall = across * rows, along * rows
    core = groups

    def image_peer(d):
        p = flipped(m, d)
        return p, {"grp": p % groups, "blk": o * inner + p // groups}

    def text_peer(d):
        p = flipped(o, d)
        return p, {"grp": g, "blk": p * inner + i}

    def block(ref, p):
        return ref.at[pl.ds(pl.multiple_of(p * rows, rows), rows)]

    def copy(src, dst, send, recv, to):
        return pltpu.make_async_remote_copy(
            src_ref=src, dst_ref=dst, send_sem=send, recv_sem=recv,
            device_id=to, device_id_type=MESH)

    near = [d for d in range(1, across) if not d & core]

    def image_copy(d):
        return copy(block(imgs, m), block(imgs, m), img_send.at[d], img_recv.at[m], image_peer(d)[1])

    def image_relay(d):
        p = flipped(m, d)
        return copy(block(imgs, p), block(imgs, p), img_send.at[d + core], img_recv.at[p],
                    image_peer(core)[1])

    def image_arrival(d):
        p = flipped(m, d)
        return copy(block(imgs, p), block(imgs, p), img_send.at[d], img_recv.at[p], image_peer(d)[1])

    def text_copy(d, arriving=False):
        p, to = text_peer(d)
        at = p if arriving else o
        return copy(block(txts, at), block(txts, at), txt_send.at[d], txt_recv.at[at], to)

    def image_sum_copy(d, arriving=False):
        p, to = image_peer(d)
        at = p if arriving else m
        return copy(img_go.at[p], img_in.at[at], ip_send.at[d], ip_recv.at[at], to)

    def text_sum_copy(d, arriving=False):
        p, to = text_peer(d)
        at = p if arriving else o
        return copy(txt_go.at[p], txt_in.at[at], tp_send.at[d], tp_recv.at[at], to)

    def loss_a_copy(d, arriving=False):
        p, to = image_peer(d)
        at = p if arriving else m
        return copy(loss_a.at[m], loss_a.at[at], la_send.at[d], la_recv.at[at], to)

    def loss_b_copy(d, arriving=False):
        p, to = text_peer(d)
        at = p if arriving else o
        return copy(loss_b.at[o], loss_b.at[at], lb_send.at[d], lb_recv.at[at], to)

    loads = [pltpu.make_async_copy(src, dst, load_sem.at[k]) for k, (src, dst) in enumerate(
        [(txt_hbm, txt_ref), (img_hbm, img_ref), (mask_hbm, mask_s), (mask_hbm, mask_v)])]
    for load in loads:
        load.start()
    barrier = pltpu.get_barrier_semaphore()
    for d in range(1, along):
        pl.semaphore_signal(barrier, inc=1, device_id=text_peer(d)[1], device_id_type=MESH)
    for d in range(1, across):
        pl.semaphore_signal(barrier, inc=1, device_id=image_peer(d)[1], device_id_type=MESH)

    loads[0].wait()
    x = txt_ref[...].astype(jnp.float32)
    block(txts, o)[...] = (x * inverse_norm(x)).astype(jnp.bfloat16)
    loads[1].wait()
    x = img_ref[...].astype(jnp.float32)
    block(imgs, m)[...] = (x * inverse_norm(x)).astype(jnp.bfloat16)
    pl.semaphore_wait(barrier, along + across - 2)

    for d in range(1, along):
        text_copy(d).start()
    for d in near + [core]:
        image_copy(d).start()
    loads[2].wait()
    loads[3].wait()
    for d in near:
        image_arrival(d).wait_recv()
        image_relay(d).start()
    for d in [core] + [d + core for d in near]:
        image_arrival(d).wait_recv()

    image_ids = o * wide + lax.broadcasted_iota(jnp.int32, (rows, wide), 1)
    iota = lax.broadcasted_iota(jnp.int32, (rows, wide), 0)
    loss = jnp.zeros((rows, TILE), jnp.float32)
    for d in range(along):
        p = flipped(o, d)
        if d:
            text_copy(d, True).wait_recv()
        logits = TEMP * lax.dot_general(
            block(txts, p)[...], imgs[...], (((1,), (1,)), ((), ())),
            preferred_element_type=jnp.float32) + BIAS
        start = ((p * inner + i) * groups + g) * rows
        held = jnp.concatenate([
            jnp.full((rows, TILE), mask_s[start // TILE, (o * wide) // TILE + j], jnp.int32)
            for j in range(wide // TILE)], axis=1)
        matched = start + iota == image_ids
        valid = (held == 0) | matched
        z = jnp.where(matched, -logits, logits)
        e = jnp.exp(-jnp.abs(logits))
        terms = jnp.where(valid, jnp.maximum(z, 0.0) + jnp.log1p(e), 0.0)
        loss += sum(terms[:, j * TILE:(j + 1) * TILE] for j in range(wide // TILE))
        sig = jnp.where(logits >= 0, 1.0, e) / (1.0 + e)
        value = jnp.where(valid, sig - matched.astype(jnp.float32), 0.0).astype(jnp.bfloat16)
        block(coef, p)[...] = value
        sums = jnp.dot(value, imgs[...], preferred_element_type=jnp.float32)
        if d:
            txt_go[p] = pack(sums)
            text_sum_copy(d).start()
        else:
            txt_part[...] = sums
    loss_a[m] = jnp.sum(loss.reshape(rows // 8, 8, TILE), axis=0)
    for d in range(1, across):
        loss_a_copy(d).start()

    img_part[...] = lax.dot_general(
        coef[...], txts[...], (((0,), (0,)), ((), ())), preferred_element_type=jnp.float32)
    for d in reversed(range(1, across)):
        p = flipped(m, d)
        img_go[p] = pack(block(img_part, p)[...])
        image_sum_copy(d).start()

    for d in range(1, across):
        loss_a_copy(d, True).wait_recv()
    loss_b[o] = jnp.sum(loss_a[...], axis=0)
    for d in range(1, along):
        loss_b_copy(d).start()

    total = txt_part[...]
    for d in range(1, along):
        text_sum_copy(d, True).wait_recv()
        total += unpack(txt_in[flipped(o, d)])
    txt_out[...] = backward(txt_ref[...].astype(jnp.float32), TEMP * total)

    for d in range(1, along):
        loss_b_copy(d, True).wait_recv()
    loss = jnp.sum(jnp.sum(loss_b[...], axis=0), keepdims=True)
    open_tiles = jnp.sum((mask_v[...] == 0).astype(jnp.float32), keepdims=True)
    loss_out[...] = loss / (open_tiles * (TILE * TILE) + (loops * groups * rows))

    total = block(img_part, m)[...]
    for d in reversed(range(1, across)):
        image_sum_copy(d, True).wait_recv()
        total += unpack(img_in[flipped(m, d)])
    img_out[...] = backward(img_ref[...].astype(jnp.float32), TEMP * total)

    for d in near:
        image_relay(d).wait_send()
    for d in near + [core]:
        image_copy(d).wait_send()
    for d in range(1, across):
        image_sum_copy(d).wait_send()
        loss_a_copy(d).wait_send()
    for d in range(1, along):
        text_copy(d).wait_send()
        text_sum_copy(d).wait_send()
        loss_b_copy(d).wait_send()


def solution(mesh):
    groups, loops = mesh.shape["grp"], mesh.shape["blk"]

    def on_device(images, texts, tile_mask):
        rows, width = images.shape
        inner = split_of(groups, loops, rows)
        across, along = groups * inner, loops // inner
        wide, tall = across * rows, along * rows
        dma = pltpu.SemaphoreType.DMA
        vmem = pl.BlockSpec(memory_space=pltpu.VMEM)
        image_grads, text_grads, loss = pl.pallas_call(
            functools.partial(kernel, groups, loops, inner),
            out_shape=(
                jax.ShapeDtypeStruct((rows, width), jnp.float32),
                jax.ShapeDtypeStruct((rows, width), jnp.float32),
                jax.ShapeDtypeStruct((1, 1), jnp.float32),
            ),
            in_specs=[pl.BlockSpec(memory_space=pltpu.HBM)] * 3,
            out_specs=(vmem, vmem, vmem),
            scratch_shapes=[
                pltpu.SMEM(tile_mask.shape, jnp.int32),
                pltpu.VMEM(tile_mask.shape, jnp.int32),
                pltpu.VMEM((rows, width), jnp.bfloat16),
                pltpu.VMEM((rows, width), jnp.bfloat16),
                pltpu.VMEM((wide, width), jnp.bfloat16),
                pltpu.VMEM((tall, width), jnp.bfloat16),
                pltpu.VMEM((tall, wide), jnp.bfloat16),
                pltpu.VMEM((wide, width), jnp.float32),
                pltpu.VMEM((rows, width), jnp.float32),
                pltpu.VMEM((across, rows // 2, width + 128), jnp.int32),
                pltpu.VMEM((along, rows // 2, width + 128), jnp.int32),
                pltpu.VMEM((across, rows // 2, width + 128), jnp.int32),
                pltpu.VMEM((along, rows // 2, width + 128), jnp.int32),
                pltpu.VMEM((across, 8, TILE), jnp.float32),
                pltpu.VMEM((along, 8, TILE), jnp.float32),
                dma((4,)),
            ] + [dma((across,)), dma((across,)), dma((along,)), dma((along,))] * 3,
            compiler_params=pltpu.CompilerParams(
                collective_id=0, has_side_effects=True, vmem_limit_bytes=48 * 2**20),
        )(tile_mask, images, texts)
        return image_grads, text_grads, loss[0, 0]

    return jax.shard_map(
        on_device,
        mesh=mesh,
        in_specs=(P(("blk", "grp"), None), P(("blk", "grp"), None), P()),
        out_specs=(P(("blk", "grp"), None), P(("blk", "grp"), None), P()),
        check_vma=False,
    )
```

```python
import functools

import jax
import jax.numpy as jnp
from jax import lax
from jax.experimental import pallas as pl
from jax.experimental.pallas import tpu as pltpu
from jax.sharding import PartitionSpec as P

TILE = 128
TEMP = 10.0
BIAS = -2.0
EPS = 1e-06
LOG_2 = 0.6931471805599453
MESH = pl.DeviceIdType.MESH


def split_of(groups, loops, rows):
    best = None
    for inner in range(1, loops + 1):
        if loops % inner or (groups * inner * rows) % TILE:
            continue
        cost = groups * inner + loops // inner
        if best is None or cost <= best[0]:
            best = (cost, inner)
    return best[1]


def inverse_norm(x):
    return lax.rsqrt(jnp.sum(x * x, axis=-1, keepdims=True) + EPS)


def backward(x, g):
    r = inverse_norm(x)
    u = x * r
    return r * (g - u * jnp.sum(u * g, axis=-1, keepdims=True))


def flipped(place, bits):
    bit = 1
    while bit <= bits:
        if bits & bit:
            place = place + bit - 2 * bit * ((place // bit) % 2)
        bit *= 2
    return place


def step_of(exponent):
    return jnp.exp((exponent - 15.0) * LOG_2)


def pack(value):
    half = value.shape[0] // 2
    most = jnp.max(jnp.abs(value), axis=-1, keepdims=True)
    exponent = jnp.floor(jnp.log(jnp.maximum(most, 1e-30)) * (1.0 / LOG_2)) + 1.0
    fixed = jnp.clip(jnp.round(value * (1.0 / step_of(exponent))), -32767.0, 32767.0)
    fixed = jnp.concatenate(
        [fixed, jnp.broadcast_to(exponent, (value.shape[0], 128))], axis=1).astype(jnp.int32)
    return fixed[:half] * 65536 + (fixed[half:] & 65535)


def unpack(words):
    low = lax.shift_right_arithmetic(lax.shift_left(words, 16), 16)
    fixed = jnp.concatenate([lax.shift_right_arithmetic(words, 16), low], axis=0).astype(jnp.float32)
    width = fixed.shape[1] - 128
    return fixed[:, :width] * step_of(fixed[:, width:width + 1])


def kernel(groups, loops, inner, mask_hbm, img_hbm, txt_hbm,
           img_out, txt_out, loss_out,
           mask_s, mask_v, img_ref, txt_ref,
           imgs, txts, coef, img_part, txt_part, img_go, txt_go, img_in, txt_in, sib_in,
           img_res, txt_res, loss_a, loss_b,
           load_sem, sib_send, sib_recv,
           img_send, img_recv, txt_send, txt_recv,
           ip_send, ip_recv, tp_send, tp_recv,
           la_send, la_recv, lb_send, lb_recv):
    rows = img_ref.shape[0]
    across = groups * inner
    along = loops // inner
    g = lax.axis_index("grp")
    b = lax.axis_index("blk")
    o, i = b // inner, b % inner
    m = i * groups + g
    wide, tall = across * rows, along * rows
    core = groups

    def image_peer(d):
        p = flipped(m, d)
        return p, {"grp": p % groups, "blk": o * inner + p // groups}

    def text_peer(d):
        p = flipped(o, d)
        return p, {"grp": g, "blk": p * inner + i}

    def block(ref, p):
        return ref.at[pl.ds(pl.multiple_of(p * rows, rows), rows)]

    def copy(src, dst, send, recv, to):
        return pltpu.make_async_remote_copy(
            src_ref=src, dst_ref=dst, send_sem=send, recv_sem=recv,
            device_id=to, device_id_type=MESH)

    near = [d for d in range(1, across) if not d & core]

    def image_copy(d):
        return copy(block(imgs, m), block(imgs, m), img_send.at[d], img_recv.at[m], image_peer(d)[1])

    def image_relay(d):
        p = flipped(m, d)
        return copy(block(imgs, p), block(imgs, p), img_send.at[d + core], img_recv.at[p],
                    image_peer(core)[1])

    def image_arrival(d):
        p = flipped(m, d)
        return copy(block(imgs, p), block(imgs, p), img_send.at[d], img_recv.at[p], image_peer(d)[1])

    even = [d for d in range(1, along) if not d & 1]

    def text_copy(d):
        return copy(block(txts, o), block(txts, o), txt_send.at[d], txt_recv.at[o], text_peer(d)[1])

    def text_relay(d):
        p = flipped(o, d)
        return copy(block(txts, p), block(txts, p), txt_send.at[d + 1], txt_recv.at[p],
                    text_peer(1)[1])

    def text_arrival(d):
        p = flipped(o, d)
        return copy(block(txts, p), block(txts, p), txt_send.at[d], txt_recv.at[p], text_peer(d)[1])

    def sibling_copy(d, arriving=False):
        p = flipped(m, d if arriving else d + core)
        return copy(block(img_part, p), sib_in.at[d], sib_send.at[d], sib_recv.at[d],
                    image_peer(core)[1])

    def image_sum_copy(d, arriving=False):
        p, to = image_peer(d)
        at = p if arriving else m
        return copy(img_go.at[p], img_in.at[at], ip_send.at[d], ip_recv.at[at], to)

    def text_sum_copy(d, arriving=False):
        p, to = text_peer(d)
        at = p if arriving else o
        return copy(txt_go.at[p], txt_in.at[at], tp_send.at[d], tp_recv.at[at], to)

    def loss_a_copy(d, arriving=False):
        p, to = image_peer(d)
        at = p if arriving else m
        return copy(loss_a.at[m], loss_a.at[at], la_send.at[d], la_recv.at[at], to)

    def loss_b_copy(d, arriving=False):
        p, to = text_peer(d)
        at = p if arriving else o
        return copy(loss_b.at[o], loss_b.at[at], lb_send.at[d], lb_recv.at[at], to)

    loads = [pltpu.make_async_copy(src, dst, load_sem.at[k]) for k, (src, dst) in enumerate(
        [(txt_hbm, txt_ref), (img_hbm, img_ref), (mask_hbm, mask_s), (mask_hbm, mask_v)])]
    for load in loads:
        load.start()
    barrier = pltpu.get_barrier_semaphore()
    for d in range(1, along):
        pl.semaphore_signal(barrier, inc=1, device_id=text_peer(d)[1], device_id_type=MESH)
    for d in range(1, across):
        pl.semaphore_signal(barrier, inc=1, device_id=image_peer(d)[1], device_id_type=MESH)

    loads[0].wait()
    x = txt_ref[...].astype(jnp.float32)
    block(txts, o)[...] = (x * inverse_norm(x)).astype(jnp.bfloat16)
    loads[1].wait()
    x = img_ref[...].astype(jnp.float32)
    block(imgs, m)[...] = (x * inverse_norm(x)).astype(jnp.bfloat16)
    pl.semaphore_wait(barrier, along + across - 2)

    for d in even + [1] * (along > 1):
        text_copy(d).start()
    for d in near[::-1] + [core]:
        image_copy(d).start()
    loads[2].wait()
    loads[3].wait()
    for d in near:
        image_arrival(d).wait_recv()
        image_relay(d).start()
    for d in even:
        text_arrival(d).wait_recv()
        text_relay(d).start()
    for d in [core] + [d + core for d in near]:
        image_arrival(d).wait_recv()

    image_ids = o * wide + lax.broadcasted_iota(jnp.int32, (rows, wide), 1)
    iota = lax.broadcasted_iota(jnp.int32, (rows, wide), 0)
    loss = jnp.zeros((rows, TILE), jnp.float32)
    for d in [0] + even + [d for d in range(along) if d & 1]:
        p = flipped(o, d)
        if d & 1:
            text_arrival(d).wait_recv()
        logits = TEMP * lax.dot_general(
            block(txts, p)[...], imgs[...], (((1,), (1,)), ((), ())),
            preferred_element_type=jnp.float32) + BIAS
        start = ((p * inner + i) * groups + g) * rows
        held = jnp.concatenate([
            jnp.full((rows, TILE), mask_s[start // TILE, (o * wide) // TILE + j], jnp.int32)
            for j in range(wide // TILE)], axis=1)
        matched = start + iota == image_ids
        valid = (held == 0) | matched
        z = jnp.where(matched, -logits, logits)
        e = jnp.exp(-jnp.abs(logits))
        terms = jnp.where(valid, jnp.maximum(z, 0.0) + jnp.log1p(e), 0.0)
        loss += sum(terms[:, j * TILE:(j + 1) * TILE] for j in range(wide // TILE))
        sig = jnp.where(logits >= 0, 1.0, e) / (1.0 + e)
        value = jnp.where(valid, sig - matched.astype(jnp.float32), 0.0).astype(jnp.bfloat16)
        block(coef, p)[...] = value
        sums = jnp.dot(value, imgs[...], preferred_element_type=jnp.float32)
        if d:
            txt_go[p] = pack(sums)
            text_sum_copy(d).start()
        else:
            txt_part[...] = sums
    loss_a[m] = jnp.sum(loss.reshape(rows // 8, 8, TILE), axis=0)
    for d in range(1, across):
        loss_a_copy(d).start()

    img_part[...] = lax.dot_general(
        coef[...], txts[...], (((0,), (0,)), ((), ())), preferred_element_type=jnp.float32)
    for d in near[::-1] + [0]:
        sibling_copy(d).start()
    for d in near[::-1]:
        p = flipped(m, d)
        sibling_copy(d, True).wait_recv()
        img_go[p] = pack(block(img_part, p)[...] + sib_in[d])
        image_sum_copy(d).start()

    for d in range(1, across):
        loss_a_copy(d, True).wait_recv()
    loss_b[o] = jnp.sum(loss_a[...], axis=0)
    for d in range(1, along):
        loss_b_copy(d).start()

    total = txt_part[...]
    for d in range(1, along):
        text_sum_copy(d, True).wait_recv()
        total += unpack(txt_in[flipped(o, d)])
    txt_res[...] = backward(txt_ref[...].astype(jnp.float32), TEMP * total)
    txt_store = pltpu.make_async_copy(txt_res, txt_out, load_sem.at[0])
    txt_store.start()

    for d in range(1, along):
        loss_b_copy(d, True).wait_recv()
    loss = jnp.sum(jnp.sum(loss_b[...], axis=0), keepdims=True)
    open_tiles = jnp.sum((mask_v[...] == 0).astype(jnp.float32), keepdims=True)
    loss_out[...] = loss / (open_tiles * (TILE * TILE) + (loops * groups * rows))

    sibling_copy(0, True).wait_recv()
    total = block(img_part, m)[...] + sib_in[0]
    for d in near[::-1]:
        image_sum_copy(d, True).wait_recv()
        total += unpack(img_in[flipped(m, d)])
    img_res[...] = backward(img_ref[...].astype(jnp.float32), TEMP * total)
    img_store = pltpu.make_async_copy(img_res, img_out, load_sem.at[1])
    img_store.start()

    for d in near:
        image_relay(d).wait_send()
        image_sum_copy(d).wait_send()
    for d in near + [core]:
        image_copy(d).wait_send()
    for d in near + [0]:
        sibling_copy(d).wait_send()
    for d in range(1, across):
        loss_a_copy(d).wait_send()
    for d in even:
        text_relay(d).wait_send()
    for d in even + [1] * (along > 1):
        text_copy(d).wait_send()
    for d in range(1, along):
        text_sum_copy(d).wait_send()
        loss_b_copy(d).wait_send()
    txt_store.wait()
    img_store.wait()


def solution(mesh):
    groups, loops = mesh.shape["grp"], mesh.shape["blk"]

    def on_device(images, texts, tile_mask):
        rows, width = images.shape
        inner = split_of(groups, loops, rows)
        across, along = groups * inner, loops // inner
        wide, tall = across * rows, along * rows
        dma = pltpu.SemaphoreType.DMA
        vmem = pl.BlockSpec(memory_space=pltpu.VMEM)
        hbm = pl.BlockSpec(memory_space=pltpu.HBM)
        image_grads, text_grads, loss = pl.pallas_call(
            functools.partial(kernel, groups, loops, inner),
            out_shape=(
                jax.ShapeDtypeStruct((rows, width), jnp.float32),
                jax.ShapeDtypeStruct((rows, width), jnp.float32),
                jax.ShapeDtypeStruct((1, 1), jnp.float32),
            ),
            in_specs=[hbm] * 3,
            out_specs=(hbm, hbm, vmem),
            scratch_shapes=[
                pltpu.SMEM(tile_mask.shape, jnp.int32),
                pltpu.VMEM(tile_mask.shape, jnp.int32),
                pltpu.VMEM((rows, width), jnp.bfloat16),
                pltpu.VMEM((rows, width), jnp.bfloat16),
                pltpu.VMEM((wide, width), jnp.bfloat16),
                pltpu.VMEM((tall, width), jnp.bfloat16),
                pltpu.VMEM((tall, wide), jnp.bfloat16),
                pltpu.VMEM((wide, width), jnp.float32),
                pltpu.VMEM((rows, width), jnp.float32),
                pltpu.VMEM((across, rows // 2, width + 128), jnp.int32),
                pltpu.VMEM((along, rows // 2, width + 128), jnp.int32),
                pltpu.VMEM((across, rows // 2, width + 128), jnp.int32),
                pltpu.VMEM((along, rows // 2, width + 128), jnp.int32),
                pltpu.VMEM((across, rows, width), jnp.float32),
                pltpu.VMEM((rows, width), jnp.float32),
                pltpu.VMEM((rows, width), jnp.float32),
                pltpu.VMEM((across, 8, TILE), jnp.float32),
                pltpu.VMEM((along, 8, TILE), jnp.float32),
                dma((4,)),
                dma((across,)),
                dma((across,)),
            ] + [dma((across,)), dma((across,)), dma((along,)), dma((along,))] * 3,
            compiler_params=pltpu.CompilerParams(
                collective_id=0, has_side_effects=True, vmem_limit_bytes=63_400_000),
        )(tile_mask, images, texts)
        return image_grads, text_grads, loss[0, 0]

    return jax.shard_map(
        on_device,
        mesh=mesh,
        in_specs=(P(("blk", "grp"), None), P(("blk", "grp"), None), P()),
        out_specs=(P(("blk", "grp"), None), P(("blk", "grp"), None), P()),
        check_vma=False,
    )
```

```python
import functools

import jax
import jax.numpy as jnp
from jax import lax
from jax.experimental import pallas as pl
from jax.experimental.pallas import tpu as pltpu
from jax.sharding import PartitionSpec as P

TILE = 128
TEMP = 10.0
BIAS = -2.0
EPS = 1e-06
LOG_2 = 0.6931471805599453
MESH = pl.DeviceIdType.MESH


def split_of(groups, loops, rows):
    best = None
    for inner in range(1, loops + 1):
        if loops % inner or (groups * inner * rows) % TILE:
            continue
        cost = groups * inner + loops // inner
        if best is None or cost <= best[0]:
            best = (cost, inner)
    return best[1]


def inverse_norm(x):
    return lax.rsqrt(jnp.sum(x * x, axis=-1, keepdims=True) + EPS)


def backward(x, g):
    r = inverse_norm(x)
    u = x * r
    return r * (g - u * jnp.sum(u * g, axis=-1, keepdims=True))


def flipped(place, bits):
    bit = 1
    while bit <= bits:
        if bits & bit:
            place = place + bit - 2 * bit * ((place // bit) % 2)
        bit *= 2
    return place


def step_of(exponent):
    return jnp.exp((exponent - 15.0) * LOG_2)


def pack(value):
    half = value.shape[0] // 2
    most = jnp.max(jnp.abs(value), axis=-1, keepdims=True)
    exponent = jnp.floor(jnp.log(jnp.maximum(most, 1e-30)) * (1.0 / LOG_2)) + 1.0
    fixed = jnp.clip(jnp.round(value * (1.0 / step_of(exponent))), -32767.0, 32767.0)
    fixed = jnp.concatenate(
        [fixed, jnp.broadcast_to(exponent, (value.shape[0], 128))], axis=1).astype(jnp.int32)
    return fixed[:half] * 65536 + (fixed[half:] & 65535)


def unpack(words):
    low = lax.shift_right_arithmetic(lax.shift_left(words, 16), 16)
    fixed = jnp.concatenate([lax.shift_right_arithmetic(words, 16), low], axis=0).astype(jnp.float32)
    width = fixed.shape[1] - 128
    return fixed[:, :width] * step_of(fixed[:, width:width + 1])


def kernel(groups, loops, inner, mask_hbm, img_hbm, txt_hbm,
           img_out, txt_out, loss_out,
           mask_s, mask_v, img_ref, txt_ref,
           imgs, imgs_t, txts, coef, img_part, txt_part, img_go, txt_go, img_in, txt_in, sib_in,
           img_res, txt_res, loss_a, loss_b,
           load_sem, sib_send, sib_recv,
           img_send, img_recv, txt_send, txt_recv,
           ip_send, ip_recv, tp_send, tp_recv,
           la_send, la_recv, lb_send, lb_recv):
    rows = img_ref.shape[0]
    across = groups * inner
    along = loops // inner
    g = lax.axis_index("grp")
    b = lax.axis_index("blk")
    o, i = b // inner, b % inner
    m = i * groups + g
    wide, tall = across * rows, along * rows
    core = groups

    def image_peer(d):
        p = flipped(m, d)
        return p, {"grp": p % groups, "blk": o * inner + p // groups}

    def text_peer(d):
        p = flipped(o, d)
        return p, {"grp": g, "blk": p * inner + i}

    def block(ref, p):
        return ref.at[pl.ds(pl.multiple_of(p * rows, rows), rows)]

    def copy(src, dst, send, recv, to):
        return pltpu.make_async_remote_copy(
            src_ref=src, dst_ref=dst, send_sem=send, recv_sem=recv,
            device_id=to, device_id_type=MESH)

    near = [d for d in range(1, across) if not d & core]

    def image_copy(d):
        return copy(block(imgs, m), block(imgs, m), img_send.at[d], img_recv.at[m], image_peer(d)[1])

    def image_relay(d):
        p = flipped(m, d)
        return copy(block(imgs, p), block(imgs, p), img_send.at[d + core], img_recv.at[p],
                    image_peer(core)[1])

    def image_arrival(d):
        p = flipped(m, d)
        return copy(block(imgs, p), block(imgs, p), img_send.at[d], img_recv.at[p], image_peer(d)[1])

    even = [d for d in range(1, along) if not d & 1]

    def text_copy(d):
        return copy(block(txts, o), block(txts, o), txt_send.at[d], txt_recv.at[o], text_peer(d)[1])

    def text_relay(d):
        p = flipped(o, d)
        return copy(block(txts, p), block(txts, p), txt_send.at[d + 1], txt_recv.at[p],
                    text_peer(1)[1])

    def text_arrival(d):
        p = flipped(o, d)
        return copy(block(txts, p), block(txts, p), txt_send.at[d], txt_recv.at[p], text_peer(d)[1])

    def sibling_copy(d, arriving=False):
        p = flipped(m, d if arriving else d + core)
        return copy(block(img_part, p), sib_in.at[d], sib_send.at[d], sib_recv.at[d],
                    image_peer(core)[1])

    def image_sum_copy(d, arriving=False):
        p, to = image_peer(d)
        at = p if arriving else m
        return copy(img_go.at[p], img_in.at[at], ip_send.at[d], ip_recv.at[at], to)

    def text_sum_copy(d, arriving=False):
        p, to = text_peer(d)
        at = p if arriving else o
        return copy(txt_go.at[p], txt_in.at[at], tp_send.at[d], tp_recv.at[at], to)

    def loss_a_copy(d, arriving=False):
        p, to = image_peer(d)
        at = p if arriving else m
        return copy(loss_a.at[m], loss_a.at[at], la_send.at[d], la_recv.at[at], to)

    def loss_b_copy(d, arriving=False):
        p, to = text_peer(d)
        at = p if arriving else o
        return copy(loss_b.at[o], loss_b.at[at], lb_send.at[d], lb_recv.at[at], to)

    loads = [pltpu.make_async_copy(src, dst, load_sem.at[k]) for k, (src, dst) in enumerate(
        [(txt_hbm, txt_ref), (img_hbm, img_ref), (mask_hbm, mask_s), (mask_hbm, mask_v)])]
    for load in loads:
        load.start()
    barrier = pltpu.get_barrier_semaphore()
    for d in range(1, along):
        pl.semaphore_signal(barrier, inc=1, device_id=text_peer(d)[1], device_id_type=MESH)
    for d in range(1, across):
        pl.semaphore_signal(barrier, inc=1, device_id=image_peer(d)[1], device_id_type=MESH)

    loads[0].wait()
    x = txt_ref[...].astype(jnp.float32)
    block(txts, o)[...] = (x * inverse_norm(x)).astype(jnp.bfloat16)
    loads[1].wait()
    x = img_ref[...].astype(jnp.float32)
    block(imgs, m)[...] = (x * inverse_norm(x)).astype(jnp.bfloat16)
    pl.semaphore_wait(barrier, along + across - 2)

    for d in even + [1] * (along > 1):
        text_copy(d).start()
    for d in near[::-1] + [core]:
        image_copy(d).start()
    loads[2].wait()
    loads[3].wait()
    for d in near:
        image_arrival(d).wait_recv()
        image_relay(d).start()
    for d in even:
        text_arrival(d).wait_recv()
        text_relay(d).start()
    for d in [core] + [d + core for d in near]:
        image_arrival(d).wait_recv()

    imgs_t[...] = imgs[...].T
    ready = [0] + even + [1] * (along > 1)
    late = [d + 1 for d in even]
    batches = [part[k:k + 4] for part in (ready, late) for k in range(0, len(part), 4)]
    iota = lax.broadcasted_iota(jnp.int32, (rows, wide), 0)
    image_ids = o * wide + lax.broadcasted_iota(jnp.int32, (rows, wide), 1)
    loss = jnp.zeros((rows, TILE), jnp.float32)
    for batch in batches:
        places = [flipped(o, d) for d in batch]
        for d in batch:
            if d & 1:
                text_arrival(d).wait_recv()
        logits = TEMP * jnp.dot(
            jnp.concatenate([block(txts, p)[...] for p in places], axis=0), imgs_t[...],
            preferred_element_type=jnp.float32) + BIAS
        held, matched = [], []
        for p in places:
            start = ((p * inner + i) * groups + g) * rows
            held.append(jnp.concatenate([
                jnp.full((rows, TILE), mask_s[start // TILE, (o * wide) // TILE + j], jnp.int32)
                for j in range(wide // TILE)], axis=1))
            matched.append((start + iota == image_ids).astype(jnp.int32))
        matched = jnp.concatenate(matched, axis=0) != 0
        valid = (jnp.concatenate(held, axis=0) == 0) | matched
        z = jnp.where(matched, -logits, logits)
        e = jnp.exp(-jnp.abs(logits))
        terms = jnp.where(valid, jnp.maximum(z, 0.0) + jnp.log1p(e), 0.0)
        loss += sum(terms[k * rows:(k + 1) * rows, j * TILE:(j + 1) * TILE]
                    for k in range(len(batch)) for j in range(wide // TILE))
        sig = jnp.where(logits >= 0, 1.0, e) / (1.0 + e)
        value = jnp.where(valid, sig - matched.astype(jnp.float32), 0.0).astype(jnp.bfloat16)
        sums = jnp.dot(value, imgs[...], preferred_element_type=jnp.float32)
        for k, (d, p) in enumerate(zip(batch, places)):
            block(coef, p)[...] = value[k * rows:(k + 1) * rows]
            part = sums[k * rows:(k + 1) * rows]
            if d:
                txt_go[p] = pack(part)
                text_sum_copy(d).start()
            else:
                txt_part[...] = part
    loss_a[m] = jnp.sum(loss.reshape(rows // 8, 8, TILE), axis=0)
    for d in range(1, across):
        loss_a_copy(d).start()

    img_part[...] = lax.dot_general(
        coef[...], txts[...], (((0,), (0,)), ((), ())), preferred_element_type=jnp.float32)
    for d in near[::-1] + [0]:
        sibling_copy(d).start()
    for d in near[::-1]:
        p = flipped(m, d)
        sibling_copy(d, True).wait_recv()
        img_go[p] = pack(block(img_part, p)[...] + sib_in[d])
        image_sum_copy(d).start()

    for d in range(1, across):
        loss_a_copy(d, True).wait_recv()
    loss_b[o] = jnp.sum(loss_a[...], axis=0)
    for d in range(1, along):
        loss_b_copy(d).start()

    total = txt_part[...]
    for d in range(1, along):
        text_sum_copy(d, True).wait_recv()
        total += unpack(txt_in[flipped(o, d)])
    txt_res[...] = backward(txt_ref[...].astype(jnp.float32), TEMP * total)
    txt_store = pltpu.make_async_copy(txt_res, txt_out, load_sem.at[0])
    txt_store.start()

    for d in range(1, along):
        loss_b_copy(d, True).wait_recv()
    loss = jnp.sum(jnp.sum(loss_b[...], axis=0), keepdims=True)
    open_tiles = jnp.sum((mask_v[...] == 0).astype(jnp.float32), keepdims=True)
    loss_out[...] = loss / (open_tiles * (TILE * TILE) + (loops * groups * rows))

    sibling_copy(0, True).wait_recv()
    total = block(img_part, m)[...] + sib_in[0]
    for d in near[::-1]:
        image_sum_copy(d, True).wait_recv()
        total += unpack(img_in[flipped(m, d)])
    img_res[...] = backward(img_ref[...].astype(jnp.float32), TEMP * total)
    img_store = pltpu.make_async_copy(img_res, img_out, load_sem.at[1])
    img_store.start()

    for d in near:
        image_relay(d).wait_send()
        image_sum_copy(d).wait_send()
    for d in near + [core]:
        image_copy(d).wait_send()
    for d in near + [0]:
        sibling_copy(d).wait_send()
    for d in range(1, across):
        loss_a_copy(d).wait_send()
    for d in even:
        text_relay(d).wait_send()
    for d in even + [1] * (along > 1):
        text_copy(d).wait_send()
    for d in range(1, along):
        text_sum_copy(d).wait_send()
        loss_b_copy(d).wait_send()
    txt_store.wait()
    img_store.wait()


def solution(mesh):
    groups, loops = mesh.shape["grp"], mesh.shape["blk"]

    def on_device(images, texts, tile_mask):
        rows, width = images.shape
        inner = split_of(groups, loops, rows)
        across, along = groups * inner, loops // inner
        wide, tall = across * rows, along * rows
        dma = pltpu.SemaphoreType.DMA
        vmem = pl.BlockSpec(memory_space=pltpu.VMEM)
        hbm = pl.BlockSpec(memory_space=pltpu.HBM)
        image_grads, text_grads, loss = pl.pallas_call(
            functools.partial(kernel, groups, loops, inner),
            out_shape=(
                jax.ShapeDtypeStruct((rows, width), jnp.float32),
                jax.ShapeDtypeStruct((rows, width), jnp.float32),
                jax.ShapeDtypeStruct((1, 1), jnp.float32),
            ),
            in_specs=[hbm] * 3,
            out_specs=(hbm, hbm, vmem),
            scratch_shapes=[
                pltpu.SMEM(tile_mask.shape, jnp.int32),
                pltpu.VMEM(tile_mask.shape, jnp.int32),
                pltpu.VMEM((rows, width), jnp.bfloat16),
                pltpu.VMEM((rows, width), jnp.bfloat16),
                pltpu.VMEM((wide, width), jnp.bfloat16),
                pltpu.VMEM((width, wide), jnp.bfloat16),
                pltpu.VMEM((tall, width), jnp.bfloat16),
                pltpu.VMEM((tall, wide), jnp.bfloat16),
                pltpu.VMEM((wide, width), jnp.float32),
                pltpu.VMEM((rows, width), jnp.float32),
                pltpu.VMEM((across, rows // 2, width + 128), jnp.int32),
                pltpu.VMEM((along, rows // 2, width + 128), jnp.int32),
                pltpu.VMEM((across, rows // 2, width + 128), jnp.int32),
                pltpu.VMEM((along, rows // 2, width + 128), jnp.int32),
                pltpu.VMEM((across, rows, width), jnp.float32),
                pltpu.VMEM((rows, width), jnp.float32),
                pltpu.VMEM((rows, width), jnp.float32),
                pltpu.VMEM((across, 8, TILE), jnp.float32),
                pltpu.VMEM((along, 8, TILE), jnp.float32),
                dma((4,)),
                dma((across,)),
                dma((across,)),
            ] + [dma((across,)), dma((across,)), dma((along,)), dma((along,))] * 3,
            compiler_params=pltpu.CompilerParams(
                collective_id=0, has_side_effects=True, vmem_limit_bytes=63_192_064),
        )(tile_mask, images, texts)
        return image_grads, text_grads, loss[0, 0]

    return jax.shard_map(
        on_device,
        mesh=mesh,
        in_specs=(P(("blk", "grp"), None), P(("blk", "grp"), None), P()),
        out_specs=(P(("blk", "grp"), None), P(("blk", "grp"), None), P()),
        check_vma=False,
    )
```

```python
import functools

import jax
import jax.numpy as jnp
from jax import lax
from jax.experimental import pallas as pl
from jax.experimental.pallas import tpu as pltpu
from jax.sharding import PartitionSpec as P

TILE = 128
TEMP = 10.0
BIAS = -2.0
EPS = 1e-06
LOG_2 = 0.6931471805599453
MESH = pl.DeviceIdType.MESH


def split_of(groups, loops, rows):
    best = None
    for inner in range(1, loops + 1):
        if loops % inner or (groups * inner * rows) % TILE:
            continue
        cost = groups * inner + loops // inner
        if best is None or cost <= best[0]:
            best = (cost, inner)
    return best[1]


def inverse_norm(x):
    return lax.rsqrt(jnp.sum(x * x, axis=-1, keepdims=True) + EPS)


def backward(x, g):
    r = inverse_norm(x)
    u = x * r
    return r * (g - u * jnp.sum(u * g, axis=-1, keepdims=True))


def flipped(place, bits):
    bit = 1
    while bit <= bits:
        if bits & bit:
            place = place + bit - 2 * bit * ((place // bit) % 2)
        bit *= 2
    return place


def step_of(exponent):
    return jnp.exp((exponent - 15.0) * LOG_2)


def pack(value):
    half = value.shape[0] // 2
    most = jnp.max(jnp.abs(value), axis=-1, keepdims=True)
    exponent = jnp.floor(jnp.log(jnp.maximum(most, 1e-30)) * (1.0 / LOG_2)) + 1.0
    fixed = jnp.clip(jnp.round(value * (1.0 / step_of(exponent))), -32767.0, 32767.0)
    fixed = jnp.concatenate(
        [fixed, jnp.broadcast_to(exponent, (value.shape[0], 128))], axis=1).astype(jnp.int32)
    return fixed[:half] * 65536 + (fixed[half:] & 65535)


def unpack(words):
    low = lax.shift_right_arithmetic(lax.shift_left(words, 16), 16)
    fixed = jnp.concatenate([lax.shift_right_arithmetic(words, 16), low], axis=0).astype(jnp.float32)
    width = fixed.shape[1] - 128
    return fixed[:, :width] * step_of(fixed[:, width:width + 1])


def kernel(groups, loops, inner, mask_hbm, img_hbm, txt_hbm,
           img_out, txt_out, loss_out,
           mask_s, mask_v, img_ref, txt_ref,
           imgs, imgs_t, txts, coef, img_part, txt_part, img_go, txt_go, img_in, txt_in, sib_in,
           img_res, txt_res, loss_a, loss_b,
           load_sem, sib_send, sib_recv,
           img_send, img_recv, txt_send, txt_recv,
           ip_send, ip_recv, tp_send, tp_recv,
           la_send, la_recv, lb_send, lb_recv):
    rows = img_ref.shape[0]
    across = groups * inner
    along = loops // inner
    g = lax.axis_index("grp")
    b = lax.axis_index("blk")
    o, i = b // inner, b % inner
    m = i * groups + g
    wide, tall = across * rows, along * rows
    core = groups

    def image_peer(d):
        p = flipped(m, d)
        return p, {"grp": p % groups, "blk": o * inner + p // groups}

    def text_peer(d):
        p = flipped(o, d)
        return p, {"grp": g, "blk": p * inner + i}

    def block(ref, p):
        return ref.at[pl.ds(pl.multiple_of(p * rows, rows), rows)]

    def copy(src, dst, send, recv, to):
        return pltpu.make_async_remote_copy(
            src_ref=src, dst_ref=dst, send_sem=send, recv_sem=recv,
            device_id=to, device_id_type=MESH)

    near = [d for d in range(1, across) if not d & core]

    def image_copy(d):
        return copy(block(imgs, m), block(imgs, m), img_send.at[d], img_recv.at[m], image_peer(d)[1])

    def image_relay(d):
        p = flipped(m, d)
        return copy(block(imgs, p), block(imgs, p), img_send.at[d + core], img_recv.at[p],
                    image_peer(core)[1])

    def image_arrival(d):
        p = flipped(m, d)
        return copy(block(imgs, p), block(imgs, p), img_send.at[d], img_recv.at[p], image_peer(d)[1])

    even = [d for d in range(1, along) if not d & 1]

    def text_copy(d):
        return copy(block(txts, o), block(txts, o), txt_send.at[d], txt_recv.at[o], text_peer(d)[1])

    def text_relay(d):
        p = flipped(o, d)
        return copy(block(txts, p), block(txts, p), txt_send.at[d + 1], txt_recv.at[p],
                    text_peer(1)[1])

    def text_arrival(d):
        p = flipped(o, d)
        return copy(block(txts, p), block(txts, p), txt_send.at[d], txt_recv.at[p], text_peer(d)[1])

    def sibling_copy(d, arriving=False):
        p = flipped(m, d if arriving else d + core)
        return copy(block(img_part, p), sib_in.at[d], sib_send.at[d], sib_recv.at[d],
                    image_peer(core)[1])

    def image_sum_copy(d, arriving=False):
        p, to = image_peer(d)
        at = p if arriving else m
        return copy(img_go.at[p], img_in.at[at], ip_send.at[d], ip_recv.at[at], to)

    def text_sum_copy(d, arriving=False):
        p, to = text_peer(d)
        at = p if arriving else o
        return copy(txt_go.at[p], txt_in.at[at], tp_send.at[d], tp_recv.at[at], to)

    def loss_a_copy(d, arriving=False):
        p, to = image_peer(d)
        at = p if arriving else m
        return copy(loss_a.at[m], loss_a.at[at], la_send.at[d], la_recv.at[at], to)

    def loss_b_copy(d, arriving=False):
        p, to = text_peer(d)
        at = p if arriving else o
        return copy(loss_b.at[o], loss_b.at[at], lb_send.at[d], lb_recv.at[at], to)

    loads = [pltpu.make_async_copy(src, dst, load_sem.at[k]) for k, (src, dst) in enumerate(
        [(txt_hbm, txt_ref), (img_hbm, img_ref), (mask_hbm, mask_s), (mask_hbm, mask_v)])]
    for load in loads:
        load.start()
    barrier = pltpu.get_barrier_semaphore()
    for d in range(1, along):
        pl.semaphore_signal(barrier, inc=1, device_id=text_peer(d)[1], device_id_type=MESH)
    for d in range(1, across):
        pl.semaphore_signal(barrier, inc=1, device_id=image_peer(d)[1], device_id_type=MESH)

    loads[0].wait()
    x = txt_ref[...].astype(jnp.float32)
    block(txts, o)[...] = (x * inverse_norm(x)).astype(jnp.bfloat16)
    loads[1].wait()
    x = img_ref[...].astype(jnp.float32)
    block(imgs, m)[...] = (x * inverse_norm(x)).astype(jnp.bfloat16)
    pl.semaphore_wait(barrier, along + across - 2)

    for d in even[::-1] + [1] * (along > 1):
        text_copy(d).start()
    for d in near[::-1] + [core]:
        image_copy(d).start()
    loads[2].wait()
    loads[3].wait()
    for d in near:
        image_arrival(d).wait_recv()
        image_relay(d).start()
    for d in even:
        text_arrival(d).wait_recv()
        text_relay(d).start()
    for d in [core] + [d + core for d in near]:
        image_arrival(d).wait_recv()

    imgs_t[...] = imgs[...].T
    ready = [0] + even
    late = [d + 1 for d in ready if d + 1 < along]
    batches = [part[k:k + 4] for part in (ready, late) for k in range(0, len(part), 4)]
    iota = lax.broadcasted_iota(jnp.int32, (rows, wide), 0)
    image_ids = o * wide + lax.broadcasted_iota(jnp.int32, (rows, wide), 1)
    loss = jnp.zeros((rows, TILE), jnp.float32)
    for batch in batches:
        places = [flipped(o, d) for d in batch]
        for d in batch:
            if d & 1:
                text_arrival(d).wait_recv()
        logits = TEMP * jnp.dot(
            jnp.concatenate([block(txts, p)[...] for p in places], axis=0), imgs_t[...],
            preferred_element_type=jnp.float32) + BIAS
        held, matched = [], []
        for p in places:
            start = ((p * inner + i) * groups + g) * rows
            held.append(jnp.concatenate([
                jnp.full((rows, TILE), mask_s[start // TILE, (o * wide) // TILE + j], jnp.int32)
                for j in range(wide // TILE)], axis=1))
            matched.append((start + iota == image_ids).astype(jnp.int32))
        matched = jnp.concatenate(matched, axis=0) != 0
        valid = (jnp.concatenate(held, axis=0) == 0) | matched
        z = jnp.where(matched, -logits, logits)
        e = jnp.exp(-jnp.abs(logits))
        terms = jnp.where(valid, jnp.maximum(z, 0.0) + jnp.log1p(e), 0.0)
        loss += sum(terms[k * rows:(k + 1) * rows, j * TILE:(j + 1) * TILE]
                    for k in range(len(batch)) for j in range(wide // TILE))
        sig = jnp.where(logits >= 0, 1.0, e) / (1.0 + e)
        value = jnp.where(valid, sig - matched.astype(jnp.float32), 0.0).astype(jnp.bfloat16)
        sums = jnp.dot(value, imgs[...], preferred_element_type=jnp.float32)
        for k, (d, p) in enumerate(zip(batch, places)):
            block(coef, p)[...] = value[k * rows:(k + 1) * rows]
            part = sums[k * rows:(k + 1) * rows]
            if d:
                txt_go[p] = pack(part)
                text_sum_copy(d).start()
            else:
                txt_part[...] = part
    loss_a[m] = jnp.sum(loss.reshape(rows // 8, 8, TILE), axis=0)
    img_part[...] = lax.dot_general(
        coef[...], txts[...], (((0,), (0,)), ((), ())), preferred_element_type=jnp.float32)
    for d in near[::-1] + [0]:
        sibling_copy(d).start()
    for d in range(1, across):
        loss_a_copy(d).start()
    for d in near[::-1]:
        p = flipped(m, d)
        sibling_copy(d, True).wait_recv()
        img_go[p] = pack(block(img_part, p)[...] + sib_in[d])
        image_sum_copy(d).start()

    for d in range(1, across):
        loss_a_copy(d, True).wait_recv()
    loss_b[o] = jnp.sum(loss_a[...], axis=0)
    for d in range(1, along):
        loss_b_copy(d).start()

    total = txt_part[...]
    for d in range(1, along):
        text_sum_copy(d, True).wait_recv()
        total += unpack(txt_in[flipped(o, d)])
    txt_res[...] = backward(txt_ref[...].astype(jnp.float32), TEMP * total)
    txt_store = pltpu.make_async_copy(txt_res, txt_out, load_sem.at[0])
    txt_store.start()

    for d in range(1, along):
        loss_b_copy(d, True).wait_recv()
    loss = jnp.sum(jnp.sum(loss_b[...], axis=0), keepdims=True)
    open_tiles = jnp.sum((mask_v[...] == 0).astype(jnp.float32), keepdims=True)
    loss_out[...] = loss / (open_tiles * (TILE * TILE) + (loops * groups * rows))

    sibling_copy(0, True).wait_recv()
    total = block(img_part, m)[...] + sib_in[0]
    for d in near[::-1]:
        image_sum_copy(d, True).wait_recv()
        total += unpack(img_in[flipped(m, d)])
    img_res[...] = backward(img_ref[...].astype(jnp.float32), TEMP * total)
    img_store = pltpu.make_async_copy(img_res, img_out, load_sem.at[1])
    img_store.start()

    for d in near:
        image_relay(d).wait_send()
        image_sum_copy(d).wait_send()
    for d in near + [core]:
        image_copy(d).wait_send()
    for d in near + [0]:
        sibling_copy(d).wait_send()
    for d in range(1, across):
        loss_a_copy(d).wait_send()
    for d in even:
        text_relay(d).wait_send()
    for d in even + [1] * (along > 1):
        text_copy(d).wait_send()
    for d in range(1, along):
        text_sum_copy(d).wait_send()
        loss_b_copy(d).wait_send()
    txt_store.wait()
    img_store.wait()


def store(first_in, second_in, first_out, second_out, sem):
    copies = [pltpu.make_async_copy(first_in, first_out, sem.at[0]),
              pltpu.make_async_copy(second_in, second_out, sem.at[1])]
    for copy in copies:
        copy.start()
    for copy in copies:
        copy.wait()


def solution(mesh):
    groups, loops = mesh.shape["grp"], mesh.shape["blk"]

    def on_device(images, texts, tile_mask):
        rows, width = images.shape
        inner = split_of(groups, loops, rows)
        across, along = groups * inner, loops // inner
        wide, tall = across * rows, along * rows
        dma = pltpu.SemaphoreType.DMA
        vmem = pl.BlockSpec(memory_space=pltpu.VMEM)
        hbm = pl.BlockSpec(memory_space=pltpu.HBM)
        image_grads, text_grads, loss = pl.pallas_call(
            functools.partial(kernel, groups, loops, inner),
            out_shape=(
                jax.ShapeDtypeStruct((rows, width), jnp.float32),
                jax.ShapeDtypeStruct((rows, width), jnp.float32),
                jax.ShapeDtypeStruct((1, 1), jnp.float32),
            ),
            in_specs=[hbm] * 3,
            out_specs=(hbm, hbm, vmem),
            scratch_shapes=[
                pltpu.SMEM(tile_mask.shape, jnp.int32),
                pltpu.VMEM(tile_mask.shape, jnp.int32),
                pltpu.VMEM((rows, width), jnp.bfloat16),
                pltpu.VMEM((rows, width), jnp.bfloat16),
                pltpu.VMEM((wide, width), jnp.bfloat16),
                pltpu.VMEM((width, wide), jnp.bfloat16),
                pltpu.VMEM((tall, width), jnp.bfloat16),
                pltpu.VMEM((tall, wide), jnp.bfloat16),
                pltpu.VMEM((wide, width), jnp.float32),
                pltpu.VMEM((rows, width), jnp.float32),
                pltpu.VMEM((across, rows // 2, width + 128), jnp.int32),
                pltpu.VMEM((along, rows // 2, width + 128), jnp.int32),
                pltpu.VMEM((across, rows // 2, width + 128), jnp.int32),
                pltpu.VMEM((along, rows // 2, width + 128), jnp.int32),
                pltpu.VMEM((across, rows, width), jnp.float32),
                pltpu.VMEM((rows, width), jnp.float32),
                pltpu.VMEM((rows, width), jnp.float32),
                pltpu.VMEM((across, 8, TILE), jnp.float32),
                pltpu.VMEM((along, 8, TILE), jnp.float32),
                dma((4,)),
                dma((across,)),
                dma((across,)),
            ] + [dma((across,)), dma((across,)), dma((along,)), dma((along,))] * 3,
            compiler_params=pltpu.CompilerParams(
                collective_id=0, has_side_effects=True, vmem_limit_bytes=63_192_064),
        )(tile_mask, images, texts)
        image_grads, text_grads = pl.pallas_call(
            store,
            out_shape=(jax.ShapeDtypeStruct((rows, width), jnp.float32),) * 2,
            in_specs=[hbm] * 2,
            out_specs=(hbm, hbm),
            scratch_shapes=[dma((2,))],
            compiler_params=pltpu.CompilerParams(vmem_limit_bytes=63_192_064),
        )(image_grads, text_grads)
        return image_grads, text_grads, loss[0, 0]

    return jax.shard_map(
        on_device,
        mesh=mesh,
        in_specs=(P(("blk", "grp"), None), P(("blk", "grp"), None), P()),
        out_specs=(P(("blk", "grp"), None), P(("blk", "grp"), None), P()),
        check_vma=False,
    )
```

```python
import functools

import jax
import jax.numpy as jnp
from jax import lax
from jax.experimental import pallas as pl
from jax.experimental.pallas import tpu as pltpu
from jax.sharding import PartitionSpec as P

TILE = 128
TEMP = 10.0
BIAS = -2.0
EPS = 1e-06
PARTS = 2
LOG_2 = 0.6931471805599453
MESH = pl.DeviceIdType.MESH


def split_of(groups, loops, rows):
    best = None
    for inner in range(1, loops + 1):
        if loops % inner or (groups * inner * rows) % TILE:
            continue
        cost = groups * inner + loops // inner
        if best is None or cost <= best[0]:
            best = (cost, inner)
    return best[1]


def inverse_norm(x):
    return lax.rsqrt(jnp.sum(x * x, axis=-1, keepdims=True) + EPS)


def backward(x, g):
    r = inverse_norm(x)
    u = x * r
    return r * (g - u * jnp.sum(u * g, axis=-1, keepdims=True))


def flipped(place, bits):
    bit = 1
    while bit <= bits:
        if bits & bit:
            place = place + bit - 2 * bit * ((place // bit) % 2)
        bit *= 2
    return place


def step_of(exponent):
    return jnp.exp((exponent - 15.0) * LOG_2)


def pack(value):
    half = value.shape[0] // 2
    most = jnp.max(jnp.abs(value), axis=-1, keepdims=True)
    exponent = jnp.floor(jnp.log(jnp.maximum(most, 1e-30)) * (1.0 / LOG_2)) + 1.0
    fixed = jnp.clip(jnp.round(value * (1.0 / step_of(exponent))), -32767.0, 32767.0)
    fixed = jnp.concatenate(
        [fixed, jnp.broadcast_to(exponent, (value.shape[0], 128))], axis=1).astype(jnp.int32)
    return fixed[:half] * 65536 + (fixed[half:] & 65535)


def unpack(words):
    low = lax.shift_right_arithmetic(lax.shift_left(words, 16), 16)
    fixed = jnp.concatenate([lax.shift_right_arithmetic(words, 16), low], axis=0).astype(jnp.float32)
    width = fixed.shape[1] - 128
    return fixed[:, :width] * step_of(fixed[:, width:width + 1])


class Copies:
    def __init__(self, parts):
        self.parts = parts

    def start(self):
        for part in self.parts:
            part.start()

    def wait_send(self):
        for part in self.parts:
            part.wait_send()

    def wait_recv(self):
        for part in self.parts:
            part.wait_recv()


def kernel(groups, loops, inner, mask_hbm, img_hbm, txt_hbm,
           img_out, txt_out, loss_out,
           mask_s, mask_v, img_ref, txt_ref,
           imgs, imgs_t, txts, coef, img_part, txt_part, img_go, txt_go, img_in, txt_in, sib_in,
           img_res, txt_res, loss_a, loss_b,
           load_sem, sib_send, sib_recv,
           img_send, img_recv, txt_send, txt_recv,
           ip_send, ip_recv, tp_send, tp_recv,
           la_send, la_recv, lb_send, lb_recv):
    rows = img_ref.shape[0]
    across = groups * inner
    along = loops // inner
    g = lax.axis_index("grp")
    b = lax.axis_index("blk")
    o, i = b // inner, b % inner
    m = i * groups + g
    wide, tall = across * rows, along * rows
    core = groups

    def image_peer(d):
        p = flipped(m, d)
        return p, {"grp": p % groups, "blk": o * inner + p // groups}

    def text_peer(d):
        p = flipped(o, d)
        return p, {"grp": g, "blk": p * inner + i}

    def block(ref, p):
        return ref.at[pl.ds(pl.multiple_of(p * rows, rows), rows)]

    def copy(src, dst, send, recv, to, parts=PARTS):
        size = src.shape[0] // parts
        return Copies([pltpu.make_async_remote_copy(
            src_ref=src.at[pl.ds(k * size, size)], dst_ref=dst.at[pl.ds(k * size, size)],
            send_sem=send.at[k], recv_sem=recv.at[k],
            device_id=to, device_id_type=MESH) for k in range(parts)])

    near = [d for d in range(1, across) if not d & core]

    def image_copy(d):
        return copy(block(imgs, m), block(imgs, m), img_send.at[d], img_recv.at[m], image_peer(d)[1])

    def image_relay(d):
        p = flipped(m, d)
        return copy(block(imgs, p), block(imgs, p), img_send.at[d + core], img_recv.at[p],
                    image_peer(core)[1])

    def image_arrival(d):
        p = flipped(m, d)
        return copy(block(imgs, p), block(imgs, p), img_send.at[d], img_recv.at[p], image_peer(d)[1])

    even = [d for d in range(1, along) if not d & 1]

    def text_copy(d):
        return copy(block(txts, o), block(txts, o), txt_send.at[d], txt_recv.at[o], text_peer(d)[1])

    def text_relay(d):
        p = flipped(o, d)
        return copy(block(txts, p), block(txts, p), txt_send.at[d + 1], txt_recv.at[p],
                    text_peer(1)[1])

    def text_arrival(d):
        p = flipped(o, d)
        return copy(block(txts, p), block(txts, p), txt_send.at[d], txt_recv.at[p], text_peer(d)[1])

    def sibling_copy(d, arriving=False):
        p = flipped(m, d if arriving else d + core)
        return copy(block(img_part, p), sib_in.at[d], sib_send.at[d], sib_recv.at[d],
                    image_peer(core)[1])

    def image_sum_copy(d, arriving=False):
        p, to = image_peer(d)
        at = p if arriving else m
        return copy(img_go.at[p], img_in.at[at], ip_send.at[d], ip_recv.at[at], to)

    def text_sum_copy(d, arriving=False):
        p, to = text_peer(d)
        at = p if arriving else o
        return copy(txt_go.at[p], txt_in.at[at], tp_send.at[d], tp_recv.at[at], to)

    def loss_a_copy(d, arriving=False):
        p, to = image_peer(d)
        at = p if arriving else m
        return copy(loss_a.at[m], loss_a.at[at], la_send.at[d], la_recv.at[at], to, 1)

    def loss_b_copy(d, arriving=False):
        p, to = text_peer(d)
        at = p if arriving else o
        return copy(loss_b.at[o], loss_b.at[at], lb_send.at[d], lb_recv.at[at], to, 1)

    loads = [pltpu.make_async_copy(src, dst, load_sem.at[k]) for k, (src, dst) in enumerate(
        [(txt_hbm, txt_ref), (img_hbm, img_ref), (mask_hbm, mask_s), (mask_hbm, mask_v)])]
    for load in loads:
        load.start()
    barrier = pltpu.get_barrier_semaphore()
    for d in range(1, along):
        pl.semaphore_signal(barrier, inc=1, device_id=text_peer(d)[1], device_id_type=MESH)
    for d in range(1, across):
        pl.semaphore_signal(barrier, inc=1, device_id=image_peer(d)[1], device_id_type=MESH)

    loads[0].wait()
    x = txt_ref[...].astype(jnp.float32)
    block(txts, o)[...] = (x * inverse_norm(x)).astype(jnp.bfloat16)
    loads[1].wait()
    x = img_ref[...].astype(jnp.float32)
    block(imgs, m)[...] = (x * inverse_norm(x)).astype(jnp.bfloat16)
    pl.semaphore_wait(barrier, along + across - 2)

    for d in even[::-1] + [1] * (along > 1):
        text_copy(d).start()
    for d in near[::-1] + [core]:
        image_copy(d).start()
    loads[2].wait()
    loads[3].wait()
    for d in near:
        for part, relay in zip(image_arrival(d).parts, image_relay(d).parts):
            part.wait_recv()
            relay.start()
    for d in even:
        for part, relay in zip(text_arrival(d).parts, text_relay(d).parts):
            part.wait_recv()
            relay.start()
    for d in [core] + [d + core for d in near]:
        image_arrival(d).wait_recv()

    imgs_t[...] = imgs[...].T
    ready = [0] + even
    late = [d + 1 for d in ready if d + 1 < along]
    batches = [part[k:k + 4] for part in (ready, late) for k in range(0, len(part), 4)]
    iota = lax.broadcasted_iota(jnp.int32, (rows, wide), 0)
    image_ids = o * wide + lax.broadcasted_iota(jnp.int32, (rows, wide), 1)
    loss = jnp.zeros((rows, TILE), jnp.float32)
    for batch in batches:
        places = [flipped(o, d) for d in batch]
        for d in batch:
            if d & 1:
                text_arrival(d).wait_recv()
        logits = TEMP * jnp.dot(
            jnp.concatenate([block(txts, p)[...] for p in places], axis=0), imgs_t[...],
            preferred_element_type=jnp.float32) + BIAS
        held, matched = [], []
        for p in places:
            start = ((p * inner + i) * groups + g) * rows
            held.append(jnp.concatenate([
                jnp.full((rows, TILE), mask_s[start // TILE, (o * wide) // TILE + j], jnp.int32)
                for j in range(wide // TILE)], axis=1))
            matched.append((start + iota == image_ids).astype(jnp.int32))
        matched = jnp.concatenate(matched, axis=0) != 0
        valid = (jnp.concatenate(held, axis=0) == 0) | matched
        z = jnp.where(matched, -logits, logits)
        e = jnp.exp(-jnp.abs(logits))
        terms = jnp.where(valid, jnp.maximum(z, 0.0) + jnp.log1p(e), 0.0)
        loss += sum(terms[k * rows:(k + 1) * rows, j * TILE:(j + 1) * TILE]
                    for k in range(len(batch)) for j in range(wide // TILE))
        sig = jnp.where(logits >= 0, 1.0, e) / (1.0 + e)
        value = jnp.where(valid, sig - matched.astype(jnp.float32), 0.0).astype(jnp.bfloat16)
        sums = jnp.dot(value, imgs[...], preferred_element_type=jnp.float32)
        for k, (d, p) in enumerate(zip(batch, places)):
            block(coef, p)[...] = value[k * rows:(k + 1) * rows]
            part = sums[k * rows:(k + 1) * rows]
            if d:
                txt_go[p] = pack(part)
                text_sum_copy(d).start()
            else:
                txt_part[...] = part
    loss_a[m] = jnp.sum(loss.reshape(rows // 8, 8, TILE), axis=0)
    img_part[...] = lax.dot_general(
        coef[...], txts[...], (((0,), (0,)), ((), ())), preferred_element_type=jnp.float32)
    for d in near[::-1] + [0]:
        sibling_copy(d).start()
    for d in range(1, across):
        loss_a_copy(d).start()
    for d in near[::-1]:
        p = flipped(m, d)
        sibling_copy(d, True).wait_recv()
        img_go[p] = pack(block(img_part, p)[...] + sib_in[d])
        image_sum_copy(d).start()

    for d in range(1, across):
        loss_a_copy(d, True).wait_recv()
    loss_b[o] = jnp.sum(loss_a[...], axis=0)
    for d in range(1, along):
        loss_b_copy(d).start()

    total = txt_part[...]
    for d in range(1, along):
        text_sum_copy(d, True).wait_recv()
        total += unpack(txt_in[flipped(o, d)])
    txt_res[...] = backward(txt_ref[...].astype(jnp.float32), TEMP * total)
    txt_store = pltpu.make_async_copy(txt_res, txt_out, load_sem.at[0])
    txt_store.start()

    for d in range(1, along):
        loss_b_copy(d, True).wait_recv()
    loss = jnp.sum(jnp.sum(loss_b[...], axis=0), keepdims=True)
    open_tiles = jnp.sum((mask_v[...] == 0).astype(jnp.float32), keepdims=True)
    loss_out[...] = loss / (open_tiles * (TILE * TILE) + (loops * groups * rows))

    sibling_copy(0, True).wait_recv()
    total = block(img_part, m)[...] + sib_in[0]
    for d in near[::-1]:
        image_sum_copy(d, True).wait_recv()
        total += unpack(img_in[flipped(m, d)])
    img_res[...] = backward(img_ref[...].astype(jnp.float32), TEMP * total)
    img_store = pltpu.make_async_copy(img_res, img_out, load_sem.at[1])
    img_store.start()

    for d in near:
        image_relay(d).wait_send()
        image_sum_copy(d).wait_send()
    for d in near + [core]:
        image_copy(d).wait_send()
    for d in near + [0]:
        sibling_copy(d).wait_send()
    for d in range(1, across):
        loss_a_copy(d).wait_send()
    for d in even:
        text_relay(d).wait_send()
    for d in even + [1] * (along > 1):
        text_copy(d).wait_send()
    for d in range(1, along):
        text_sum_copy(d).wait_send()
        loss_b_copy(d).wait_send()
    txt_store.wait()
    img_store.wait()


def solution(mesh):
    groups, loops = mesh.shape["grp"], mesh.shape["blk"]

    def on_device(images, texts, tile_mask):
        rows, width = images.shape
        inner = split_of(groups, loops, rows)
        across, along = groups * inner, loops // inner
        wide, tall = across * rows, along * rows
        dma = pltpu.SemaphoreType.DMA
        vmem = pl.BlockSpec(memory_space=pltpu.VMEM)
        hbm = pl.BlockSpec(memory_space=pltpu.HBM)
        image_grads, text_grads, loss = pl.pallas_call(
            functools.partial(kernel, groups, loops, inner),
            out_shape=(
                jax.ShapeDtypeStruct((rows, width), jnp.float32),
                jax.ShapeDtypeStruct((rows, width), jnp.float32),
                jax.ShapeDtypeStruct((1, 1), jnp.float32),
            ),
            in_specs=[hbm] * 3,
            out_specs=(hbm, hbm, vmem),
            scratch_shapes=[
                pltpu.SMEM(tile_mask.shape, jnp.int32),
                pltpu.VMEM(tile_mask.shape, jnp.int32),
                pltpu.VMEM((rows, width), jnp.bfloat16),
                pltpu.VMEM((rows, width), jnp.bfloat16),
                pltpu.VMEM((wide, width), jnp.bfloat16),
                pltpu.VMEM((width, wide), jnp.bfloat16),
                pltpu.VMEM((tall, width), jnp.bfloat16),
                pltpu.VMEM((tall, wide), jnp.bfloat16),
                pltpu.VMEM((wide, width), jnp.float32),
                pltpu.VMEM((rows, width), jnp.float32),
                pltpu.VMEM((across, rows // 2, width + 128), jnp.int32),
                pltpu.VMEM((along, rows // 2, width + 128), jnp.int32),
                pltpu.VMEM((across, rows // 2, width + 128), jnp.int32),
                pltpu.VMEM((along, rows // 2, width + 128), jnp.int32),
                pltpu.VMEM((across, rows, width), jnp.float32),
                pltpu.VMEM((rows, width), jnp.float32),
                pltpu.VMEM((rows, width), jnp.float32),
                pltpu.VMEM((across, 8, TILE), jnp.float32),
                pltpu.VMEM((along, 8, TILE), jnp.float32),
                dma((4,)),
                dma((across, PARTS)),
                dma((across, PARTS)),
            ] + [dma((across, PARTS)), dma((across, PARTS)), dma((along, PARTS)), dma((along, PARTS))] * 3,
            compiler_params=pltpu.CompilerParams(
                collective_id=0, has_side_effects=True, vmem_limit_bytes=63_123_000),
        )(tile_mask, images, texts)
        return image_grads, text_grads, loss[0, 0]

    return jax.shard_map(
        on_device,
        mesh=mesh,
        in_specs=(P(("blk", "grp"), None), P(("blk", "grp"), None), P()),
        out_specs=(P(("blk", "grp"), None), P(("blk", "grp"), None), P()),
        check_vma=False,
    )
```

```python
import functools

import jax
import jax.numpy as jnp
from jax import lax
from jax.experimental import pallas as pl
from jax.experimental.pallas import tpu as pltpu
from jax.sharding import PartitionSpec as P

TILE = 128
TEMP = 10.0
BIAS = -2.0
EPS = 1e-06
LOG_2 = 0.6931471805599453
MESH = pl.DeviceIdType.MESH


def split_of(groups, loops, rows):
    best = None
    for inner in range(1, loops + 1):
        if loops % inner or (groups * inner * rows) % TILE:
            continue
        cost = groups * inner + loops // inner
        if best is None or cost <= best[0]:
            best = (cost, inner)
    return best[1]


def inverse_norm(x):
    return lax.rsqrt(jnp.sum(x * x, axis=-1, keepdims=True) + EPS)


def backward(x, g):
    r = inverse_norm(x)
    u = x * r
    return r * (g - u * jnp.sum(u * g, axis=-1, keepdims=True))


def flipped(place, bits):
    bit = 1
    while bit <= bits:
        if bits & bit:
            place = place + bit - 2 * bit * ((place // bit) % 2)
        bit *= 2
    return place


def step_of(exponent):
    return jnp.exp((exponent - 15.0) * LOG_2)


def pack(value):
    half = value.shape[0] // 2
    most = jnp.max(jnp.abs(value), axis=-1, keepdims=True)
    exponent = jnp.floor(jnp.log(jnp.maximum(most, 1e-30)) * (1.0 / LOG_2)) + 1.0
    fixed = jnp.clip(jnp.round(value * (1.0 / step_of(exponent))), -32767.0, 32767.0)
    fixed = jnp.concatenate(
        [fixed, jnp.broadcast_to(exponent, (value.shape[0], 128))], axis=1).astype(jnp.int32)
    return fixed[:half] * 65536 + (fixed[half:] & 65535)


def unpack(words):
    low = lax.shift_right_arithmetic(lax.shift_left(words, 16), 16)
    fixed = jnp.concatenate([lax.shift_right_arithmetic(words, 16), low], axis=0).astype(jnp.float32)
    width = fixed.shape[1] - 128
    return fixed[:, :width] * step_of(fixed[:, width:width + 1])


def kernel(groups, loops, inner, mask_hbm, img_hbm, txt_hbm,
           img_out, txt_out, loss_out,
           mask_s, mask_v, img_ref, txt_ref,
           imgs, imgs_t, txts, coef, img_part, txt_part, img_go, txt_go, img_in, txt_in, sib_in,
           img_res, txt_res, loss_a, loss_b,
           load_sem, sib_send, sib_recv,
           img_send, img_recv, txt_send, txt_recv,
           ip_send, ip_recv, tp_send, tp_recv,
           la_send, la_recv, lb_send, lb_recv):
    rows = img_ref.shape[0]
    across = groups * inner
    along = loops // inner
    g = lax.axis_index("grp")
    b = lax.axis_index("blk")
    o, i = b // inner, b % inner
    m = i * groups + g
    wide, tall = across * rows, along * rows
    core = groups

    def image_peer(d):
        p = flipped(m, d)
        return p, {"grp": p % groups, "blk": o * inner + p // groups}

    def text_peer(d):
        p = flipped(o, d)
        return p, {"grp": g, "blk": p * inner + i}

    def block(ref, p):
        return ref.at[pl.ds(pl.multiple_of(p * rows, rows), rows)]

    def copy(src, dst, send, recv, to):
        return pltpu.make_async_remote_copy(
            src_ref=src, dst_ref=dst, send_sem=send, recv_sem=recv,
            device_id=to, device_id_type=MESH)

    near = [d for d in range(1, across) if not d & core]

    def image_copy(d):
        return copy(block(imgs, m), block(imgs, m), img_send.at[d], img_recv.at[m], image_peer(d)[1])

    def image_relay(d):
        p = flipped(m, d)
        return copy(block(imgs, p), block(imgs, p), img_send.at[d + core], img_recv.at[p],
                    image_peer(core)[1])

    def image_arrival(d):
        p = flipped(m, d)
        return copy(block(imgs, p), block(imgs, p), img_send.at[d], img_recv.at[p], image_peer(d)[1])

    even = [d for d in range(1, along) if not d & 1]

    def text_copy(d):
        return copy(block(txts, o), block(txts, o), txt_send.at[d], txt_recv.at[o], text_peer(d)[1])

    def text_relay(d):
        p = flipped(o, d)
        return copy(block(txts, p), block(txts, p), txt_send.at[d + 1], txt_recv.at[p],
                    text_peer(1)[1])

    def text_arrival(d):
        p = flipped(o, d)
        return copy(block(txts, p), block(txts, p), txt_send.at[d], txt_recv.at[p], text_peer(d)[1])

    def sibling_copy(d, arriving=False):
        p = flipped(m, d if arriving else d + core)
        return copy(block(img_part, p), sib_in.at[d], sib_send.at[d], sib_recv.at[d],
                    image_peer(core)[1])

    def image_sum_copy(d, arriving=False):
        p, to = image_peer(d)
        at = p if arriving else m
        return copy(img_go.at[p], img_in.at[at], ip_send.at[d], ip_recv.at[at], to)

    def text_sum_copy(d, arriving=False):
        p, to = text_peer(d)
        at = p if arriving else o
        return copy(txt_go.at[p], txt_in.at[at], tp_send.at[d], tp_recv.at[at], to)

    def loss_a_copy(d, arriving=False):
        p, to = image_peer(d)
        at = p if arriving else m
        return copy(loss_a.at[m], loss_a.at[at], la_send.at[d], la_recv.at[at], to)

    def loss_b_copy(d, arriving=False):
        p, to = text_peer(d)
        at = p if arriving else o
        return copy(loss_b.at[o], loss_b.at[at], lb_send.at[d], lb_recv.at[at], to)

    loads = [pltpu.make_async_copy(src, dst, load_sem.at[k]) for k, (src, dst) in enumerate(
        [(txt_hbm, txt_ref), (img_hbm, img_ref), (mask_hbm, mask_s), (mask_hbm, mask_v)])]
    for load in loads:
        load.start()
    barrier = pltpu.get_barrier_semaphore()
    for d in range(1, along):
        pl.semaphore_signal(barrier, inc=1, device_id=text_peer(d)[1], device_id_type=MESH)
    for d in range(1, across):
        pl.semaphore_signal(barrier, inc=1, device_id=image_peer(d)[1], device_id_type=MESH)

    loads[0].wait()
    x = txt_ref[...].astype(jnp.float32)
    block(txts, o)[...] = (x * inverse_norm(x)).astype(jnp.bfloat16)
    loads[1].wait()
    x = img_ref[...].astype(jnp.float32)
    block(imgs, m)[...] = (x * inverse_norm(x)).astype(jnp.bfloat16)
    pl.semaphore_wait(barrier, along + across - 2)

    for d in even[::-1] + [1] * (along > 1):
        text_copy(d).start()
    for d in near[::-1] + [core]:
        image_copy(d).start()
    loads[2].wait()
    loads[3].wait()
    for d in near:
        image_arrival(d).wait_recv()
        image_relay(d).start()
    for d in even:
        text_arrival(d).wait_recv()
        text_relay(d).start()
    for d in [core] + [d + core for d in near]:
        image_arrival(d).wait_recv()

    imgs_t[...] = imgs[...].T
    ready = [0] + even
    late = [d + 1 for d in ready if d + 1 < along]
    batches = [part[k:k + 4] for part in (ready, late) for k in range(0, len(part), 4)]
    iota = lax.broadcasted_iota(jnp.int32, (rows, wide), 0)
    image_ids = o * wide + lax.broadcasted_iota(jnp.int32, (rows, wide), 1)
    loss = jnp.zeros((rows, TILE), jnp.float32)

    def send_text_sums(batch, value):
        sums = jnp.dot(value, imgs[...], preferred_element_type=jnp.float32)
        for k, d in enumerate(batch):
            part = sums[k * rows:(k + 1) * rows]
            if d:
                txt_go[flipped(o, d)] = pack(part)
                text_sum_copy(d).start()
            else:
                txt_part[...] = part

    for batch in batches:
        places = [flipped(o, d) for d in batch]
        for d in batch:
            if d & 1:
                text_arrival(d).wait_recv()
        logits = TEMP * jnp.dot(
            jnp.concatenate([block(txts, p)[...] for p in places], axis=0), imgs_t[...],
            preferred_element_type=jnp.float32) + BIAS
        held, matched = [], []
        for p in places:
            start = ((p * inner + i) * groups + g) * rows
            held.append(jnp.concatenate([
                jnp.full((rows, TILE), mask_s[start // TILE, (o * wide) // TILE + j], jnp.int32)
                for j in range(wide // TILE)], axis=1))
            matched.append((start + iota == image_ids).astype(jnp.int32))
        matched = jnp.concatenate(matched, axis=0) != 0
        valid = (jnp.concatenate(held, axis=0) == 0) | matched
        z = jnp.where(matched, -logits, logits)
        e = jnp.exp(-jnp.abs(logits))
        terms = jnp.where(valid, jnp.maximum(z, 0.0) + jnp.log1p(e), 0.0)
        loss += sum(terms[k * rows:(k + 1) * rows, j * TILE:(j + 1) * TILE]
                    for k in range(len(batch)) for j in range(wide // TILE))
        sig = jnp.where(logits >= 0, 1.0, e) / (1.0 + e)
        value = jnp.where(valid, sig - matched.astype(jnp.float32), 0.0).astype(jnp.bfloat16)
        for k, p in enumerate(places):
            block(coef, p)[...] = value[k * rows:(k + 1) * rows]
        if batch is not batches[-1]:
            send_text_sums(batch, value)
    loss_a[m] = jnp.sum(loss.reshape(rows // 8, 8, TILE), axis=0)
    half = across // 2
    for far in (1, 0):
        at = flipped(m, far * half) // half * half * rows
        at = pl.multiple_of(at, half * rows)
        img_part[pl.ds(at, half * rows)] = lax.dot_general(
            coef[:, pl.ds(at, half * rows)], txts[...], (((0,), (0,)), ((), ())),
            preferred_element_type=jnp.float32)
        for d in near[::-1] + [0]:
            if (d >= half) == bool(far):
                sibling_copy(d).start()
    send_text_sums(batches[-1], value)
    for d in range(1, across):
        loss_a_copy(d).start()
    for d in near[::-1]:
        p = flipped(m, d)
        sibling_copy(d, True).wait_recv()
        img_go[p] = pack(block(img_part, p)[...] + sib_in[d])
        image_sum_copy(d).start()

    for d in range(1, across):
        loss_a_copy(d, True).wait_recv()
    loss_b[o] = jnp.sum(loss_a[...], axis=0)
    for d in range(1, along):
        loss_b_copy(d).start()

    total = txt_part[...]
    for d in range(1, along):
        text_sum_copy(d, True).wait_recv()
        total += unpack(txt_in[flipped(o, d)])
    txt_res[...] = backward(txt_ref[...].astype(jnp.float32), TEMP * total)
    txt_store = pltpu.make_async_copy(txt_res, txt_out, load_sem.at[0])
    txt_store.start()

    sibling_copy(0, True).wait_recv()
    total = block(img_part, m)[...] + sib_in[0]
    for d in near[::-1]:
        image_sum_copy(d, True).wait_recv()
        total += unpack(img_in[flipped(m, d)])
    img_res[...] = backward(img_ref[...].astype(jnp.float32), TEMP * total)
    img_store = pltpu.make_async_copy(img_res, img_out, load_sem.at[1])
    img_store.start()

    for d in range(1, along):
        loss_b_copy(d, True).wait_recv()
    loss = jnp.sum(jnp.sum(loss_b[...], axis=0), keepdims=True)
    open_tiles = jnp.sum((mask_v[...] == 0).astype(jnp.float32), keepdims=True)
    loss_out[...] = loss / (open_tiles * (TILE * TILE) + (loops * groups * rows))

    for d in near:
        image_relay(d).wait_send()
        image_sum_copy(d).wait_send()
    for d in near + [core]:
        image_copy(d).wait_send()
    for d in near + [0]:
        sibling_copy(d).wait_send()
    for d in range(1, across):
        loss_a_copy(d).wait_send()
    for d in even:
        text_relay(d).wait_send()
    for d in even + [1] * (along > 1):
        text_copy(d).wait_send()
    for d in range(1, along):
        text_sum_copy(d).wait_send()
        loss_b_copy(d).wait_send()
    txt_store.wait()
    img_store.wait()


def solution(mesh):
    groups, loops = mesh.shape["grp"], mesh.shape["blk"]

    def on_device(images, texts, tile_mask):
        rows, width = images.shape
        inner = split_of(groups, loops, rows)
        across, along = groups * inner, loops // inner
        wide, tall = across * rows, along * rows
        dma = pltpu.SemaphoreType.DMA
        vmem = pl.BlockSpec(memory_space=pltpu.VMEM)
        hbm = pl.BlockSpec(memory_space=pltpu.HBM)
        image_grads, text_grads, loss = pl.pallas_call(
            functools.partial(kernel, groups, loops, inner),
            out_shape=(
                jax.ShapeDtypeStruct((rows, width), jnp.float32),
                jax.ShapeDtypeStruct((rows, width), jnp.float32),
                jax.ShapeDtypeStruct((1, 1), jnp.float32),
            ),
            in_specs=[hbm] * 3,
            out_specs=(hbm, hbm, vmem),
            scratch_shapes=[
                pltpu.SMEM(tile_mask.shape, jnp.int32),
                pltpu.VMEM(tile_mask.shape, jnp.int32),
                pltpu.VMEM((rows, width), jnp.bfloat16),
                pltpu.VMEM((rows, width), jnp.bfloat16),
                pltpu.VMEM((wide, width), jnp.bfloat16),
                pltpu.VMEM((width, wide), jnp.bfloat16),
                pltpu.VMEM((tall, width), jnp.bfloat16),
                pltpu.VMEM((tall, wide), jnp.bfloat16),
                pltpu.VMEM((wide, width), jnp.float32),
                pltpu.VMEM((rows, width), jnp.float32),
                pltpu.VMEM((across, rows // 2, width + 128), jnp.int32),
                pltpu.VMEM((along, rows // 2, width + 128), jnp.int32),
                pltpu.VMEM((across, rows // 2, width + 128), jnp.int32),
                pltpu.VMEM((along, rows // 2, width + 128), jnp.int32),
                pltpu.VMEM((across, rows, width), jnp.float32),
                pltpu.VMEM((rows, width), jnp.float32),
                pltpu.VMEM((rows, width), jnp.float32),
                pltpu.VMEM((across, 8, TILE), jnp.float32),
                pltpu.VMEM((along, 8, TILE), jnp.float32),
                dma((4,)),
                dma((across,)),
                dma((across,)),
            ] + [dma((across,)), dma((across,)), dma((along,)), dma((along,))] * 3,
            compiler_params=pltpu.CompilerParams(
                collective_id=0, has_side_effects=True, vmem_limit_bytes=63_192_064),
        )(tile_mask, images, texts)
        return image_grads, text_grads, loss[0, 0]

    return jax.shard_map(
        on_device,
        mesh=mesh,
        in_specs=(P(("blk", "grp"), None), P(("blk", "grp"), None), P()),
        out_specs=(P(("blk", "grp"), None), P(("blk", "grp"), None), P()),
        check_vma=False,
    )
```

```python
import functools

import jax
import jax.numpy as jnp
from jax import lax
from jax.experimental import pallas as pl
from jax.experimental.pallas import tpu as pltpu
from jax.sharding import PartitionSpec as P

TILE = 128
TEMP = 10.0
BIAS = -2.0
EPS = 1e-06
LOG_2 = 0.6931471805599453
MESH = pl.DeviceIdType.MESH


def split_of(groups, loops, rows):
    best = None
    for inner in range(1, loops + 1):
        if loops % inner or (groups * inner * rows) % TILE:
            continue
        cost = groups * inner + loops // inner
        if best is None or cost <= best[0]:
            best = (cost, inner)
    return best[1]


def inverse_norm(x):
    return lax.rsqrt(jnp.sum(x * x, axis=-1, keepdims=True) + EPS)


def backward(x, g):
    r = inverse_norm(x)
    u = x * r
    return r * (g - u * jnp.sum(u * g, axis=-1, keepdims=True))


def flipped(place, bits):
    bit = 1
    while bit <= bits:
        if bits & bit:
            place = place + bit - 2 * bit * ((place // bit) % 2)
        bit *= 2
    return place


def step_of(exponent):
    return jnp.exp((exponent - 15.0) * LOG_2)


def pack(value):
    half = value.shape[0] // 2
    most = jnp.max(jnp.abs(value), axis=-1, keepdims=True)
    exponent = jnp.floor(jnp.log(jnp.maximum(most, 1e-30)) * (1.0 / LOG_2)) + 1.0
    fixed = jnp.clip(jnp.round(value * (1.0 / step_of(exponent))), -32767.0, 32767.0)
    fixed = jnp.concatenate(
        [fixed, jnp.broadcast_to(exponent, (value.shape[0], 128))], axis=1).astype(jnp.int32)
    return fixed[:half] * 65536 + (fixed[half:] & 65535)


def unpack(words):
    low = lax.shift_right_arithmetic(lax.shift_left(words, 16), 16)
    fixed = jnp.concatenate([lax.shift_right_arithmetic(words, 16), low], axis=0).astype(jnp.float32)
    width = fixed.shape[1] - 128
    return fixed[:, :width] * step_of(fixed[:, width:width + 1])


def kernel(groups, loops, inner, mask_s, both_ref,
           img_out, txt_out, loss_out,
           imgs, imgs_t, txts, coef, img_part, txt_part, img_go, txt_go, img_in, txt_in, sib_in,
           loss_a, loss_b,
           sib_send, sib_recv,
           img_send, img_recv, txt_send, txt_recv,
           ip_send, ip_recv, tp_send, tp_recv,
           la_send, la_recv, lb_send, lb_recv):
    rows = both_ref.shape[0] // 2
    img_ref, txt_ref = both_ref.at[pl.ds(0, rows)], both_ref.at[pl.ds(rows, rows)]
    across = groups * inner
    along = loops // inner
    g = lax.axis_index("grp")
    b = lax.axis_index("blk")
    o, i = b // inner, b % inner
    m = i * groups + g
    wide, tall = across * rows, along * rows
    core = groups

    def image_peer(d):
        p = flipped(m, d)
        return p, {"grp": p % groups, "blk": o * inner + p // groups}

    def text_peer(d):
        p = flipped(o, d)
        return p, {"grp": g, "blk": p * inner + i}

    def block(ref, p):
        return ref.at[pl.ds(pl.multiple_of(p * rows, rows), rows)]

    def copy(src, dst, send, recv, to):
        return pltpu.make_async_remote_copy(
            src_ref=src, dst_ref=dst, send_sem=send, recv_sem=recv,
            device_id=to, device_id_type=MESH)

    near = [d for d in range(1, across) if not d & core]

    def image_copy(d):
        return copy(block(imgs, m), block(imgs, m), img_send.at[d], img_recv.at[m], image_peer(d)[1])

    def image_relay(d):
        p = flipped(m, d)
        return copy(block(imgs, p), block(imgs, p), img_send.at[d + core], img_recv.at[p],
                    image_peer(core)[1])

    def image_arrival(d):
        p = flipped(m, d)
        return copy(block(imgs, p), block(imgs, p), img_send.at[d], img_recv.at[p], image_peer(d)[1])

    even = [d for d in range(1, along) if not d & 1]

    def text_copy(d):
        return copy(block(txts, o), block(txts, o), txt_send.at[d], txt_recv.at[o], text_peer(d)[1])

    def text_relay(d):
        p = flipped(o, d)
        return copy(block(txts, p), block(txts, p), txt_send.at[d + 1], txt_recv.at[p],
                    text_peer(1)[1])

    def text_arrival(d):
        p = flipped(o, d)
        return copy(block(txts, p), block(txts, p), txt_send.at[d], txt_recv.at[p], text_peer(d)[1])

    def sibling_copy(d, arriving=False):
        p = flipped(m, d if arriving else d + core)
        return copy(block(img_part, p), sib_in.at[d], sib_send.at[d], sib_recv.at[d],
                    image_peer(core)[1])

    def image_sum_copy(d, arriving=False):
        p, to = image_peer(d)
        at = p if arriving else m
        return copy(img_go.at[p], img_in.at[at], ip_send.at[d], ip_recv.at[at], to)

    def text_sum_copy(d, arriving=False):
        p, to = text_peer(d)
        at = p if arriving else o
        return copy(txt_go.at[p], txt_in.at[at], tp_send.at[d], tp_recv.at[at], to)

    def loss_a_copy(d, arriving=False):
        p, to = image_peer(d)
        at = p if arriving else m
        return copy(loss_a.at[m], loss_a.at[at], la_send.at[d], la_recv.at[at], to)

    def loss_b_copy(d, arriving=False):
        p, to = text_peer(d)
        at = p if arriving else o
        return copy(loss_b.at[o], loss_b.at[at], lb_send.at[d], lb_recv.at[at], to)

    barrier = pltpu.get_barrier_semaphore()
    for d in range(1, along):
        pl.semaphore_signal(barrier, inc=1, device_id=text_peer(d)[1], device_id_type=MESH)
    for d in range(1, across):
        pl.semaphore_signal(barrier, inc=1, device_id=image_peer(d)[1], device_id_type=MESH)

    x = txt_ref[...].astype(jnp.float32)
    block(txts, o)[...] = (x * inverse_norm(x)).astype(jnp.bfloat16)
    x = img_ref[...].astype(jnp.float32)
    block(imgs, m)[...] = (x * inverse_norm(x)).astype(jnp.bfloat16)
    pl.semaphore_wait(barrier, along + across - 2)

    for d in even[::-1] + [1] * (along > 1):
        text_copy(d).start()
    for d in near[::-1] + [core]:
        image_copy(d).start()
    for d in near:
        image_arrival(d).wait_recv()
        image_relay(d).start()
    for d in even:
        text_arrival(d).wait_recv()
        text_relay(d).start()
    for d in [core] + [d + core for d in near]:
        image_arrival(d).wait_recv()

    imgs_t[...] = imgs[...].T
    ready = [0] + even
    late = [d + 1 for d in ready if d + 1 < along]
    batches = [part[k:k + 4] for part in (ready, late) for k in range(0, len(part), 4)]
    iota = lax.broadcasted_iota(jnp.int32, (rows, wide), 0)
    image_ids = o * wide + lax.broadcasted_iota(jnp.int32, (rows, wide), 1)
    loss = jnp.zeros((rows, TILE), jnp.float32)
    open_tiles = jnp.int32(0)

    def send_text_sums(batch, value):
        sums = jnp.dot(value, imgs[...], preferred_element_type=jnp.float32)
        for k, d in enumerate(batch):
            part = sums[k * rows:(k + 1) * rows]
            if d:
                txt_go[flipped(o, d)] = pack(part)
                text_sum_copy(d).start()
            else:
                txt_part[...] = part

    for batch in batches:
        places = [flipped(o, d) for d in batch]
        for d in batch:
            if d & 1:
                text_arrival(d).wait_recv()
        logits = TEMP * jnp.dot(
            jnp.concatenate([block(txts, p)[...] for p in places], axis=0), imgs_t[...],
            preferred_element_type=jnp.float32) + BIAS
        held, matched = [], []
        for p in places:
            start = ((p * inner + i) * groups + g) * rows
            marks = [mask_s[start // TILE, (o * wide) // TILE + j] for j in range(wide // TILE)]
            open_tiles += sum(jnp.where(mark == 0, 1, 0) for mark in marks)
            held.append(jnp.concatenate(
                [jnp.full((rows, TILE), mark, jnp.int32) for mark in marks], axis=1))
            matched.append((start + iota == image_ids).astype(jnp.int32))
        matched = jnp.concatenate(matched, axis=0) != 0
        valid = (jnp.concatenate(held, axis=0) == 0) | matched
        z = jnp.where(matched, -logits, logits)
        e = jnp.exp(-jnp.abs(logits))
        terms = jnp.where(valid, jnp.maximum(z, 0.0) + jnp.log1p(e), 0.0)
        loss += sum(terms[k * rows:(k + 1) * rows, j * TILE:(j + 1) * TILE]
                    for k in range(len(batch)) for j in range(wide // TILE))
        sig = jnp.where(logits >= 0, 1.0, e) / (1.0 + e)
        value = jnp.where(valid, sig - matched.astype(jnp.float32), 0.0).astype(jnp.bfloat16)
        for k, p in enumerate(places):
            block(coef, p)[...] = value[k * rows:(k + 1) * rows]
        if batch is not batches[-1]:
            send_text_sums(batch, value)
    loss_a[m, 0:8] = jnp.sum(loss.reshape(rows // 8, 8, TILE), axis=0)
    loss_a[m, 8:16] = jnp.full((8, TILE), open_tiles * (rows * TILE), jnp.int32).astype(jnp.float32)
    half = across // 2
    for far in (1, 0):
        at = flipped(m, far * half) // half * half * rows
        at = pl.multiple_of(at, half * rows)
        img_part[pl.ds(at, half * rows)] = lax.dot_general(
            coef[:, pl.ds(at, half * rows)], txts[...], (((0,), (0,)), ((), ())),
            preferred_element_type=jnp.float32)
        for d in near[::-1] + [0]:
            if (d >= half) == bool(far):
                sibling_copy(d).start()
    send_text_sums(batches[-1], value)
    for d in range(1, across):
        loss_a_copy(d).start()
    for d in near[::-1]:
        p = flipped(m, d)
        sibling_copy(d, True).wait_recv()
        img_go[p] = pack(block(img_part, p)[...] + sib_in[d])
        image_sum_copy(d).start()

    for d in range(1, across):
        loss_a_copy(d, True).wait_recv()
    loss_b[o] = jnp.sum(loss_a[...], axis=0)
    for d in range(1, along):
        loss_b_copy(d).start()

    total = txt_part[...]
    for d in range(1, along):
        text_sum_copy(d, True).wait_recv()
        total += unpack(txt_in[flipped(o, d)])
    txt_out[...] = backward(txt_ref[...].astype(jnp.float32), TEMP * total)

    sibling_copy(0, True).wait_recv()
    total = block(img_part, m)[...] + sib_in[0]
    for d in near[::-1]:
        image_sum_copy(d, True).wait_recv()
        total += unpack(img_in[flipped(m, d)])
    img_out[...] = backward(img_ref[...].astype(jnp.float32), TEMP * total)

    for d in range(1, along):
        loss_b_copy(d, True).wait_recv()
    total = jnp.sum(loss_b[...], axis=0)
    loss_out[...] = jnp.sum(total[0:8], keepdims=True) / (total[8:9, 0:1] + (loops * groups * rows))

    for d in near:
        image_relay(d).wait_send()
        image_sum_copy(d).wait_send()
    for d in near + [core]:
        image_copy(d).wait_send()
    for d in near + [0]:
        sibling_copy(d).wait_send()
    for d in range(1, across):
        loss_a_copy(d).wait_send()
    for d in even:
        text_relay(d).wait_send()
    for d in even + [1] * (along > 1):
        text_copy(d).wait_send()
    for d in range(1, along):
        text_sum_copy(d).wait_send()
        loss_b_copy(d).wait_send()


def solution(mesh):
    groups, loops = mesh.shape["grp"], mesh.shape["blk"]

    def on_device(images, texts, tile_mask):
        rows, width = images.shape
        inner = split_of(groups, loops, rows)
        across, along = groups * inner, loops // inner
        wide, tall = across * rows, along * rows
        dma = pltpu.SemaphoreType.DMA
        vmem = pl.BlockSpec(memory_space=pltpu.VMEM)
        image_grads, text_grads, loss = pl.pallas_call(
            functools.partial(kernel, groups, loops, inner),
            out_shape=(
                jax.ShapeDtypeStruct((rows, width), jnp.float32),
                jax.ShapeDtypeStruct((rows, width), jnp.float32),
                jax.ShapeDtypeStruct((1, 1), jnp.float32),
            ),
            in_specs=[pl.BlockSpec(memory_space=pltpu.SMEM), vmem],
            out_specs=(vmem, vmem, vmem),
            scratch_shapes=[
                pltpu.VMEM((wide, width), jnp.bfloat16),
                pltpu.VMEM((width, wide), jnp.bfloat16),
                pltpu.VMEM((tall, width), jnp.bfloat16),
                pltpu.VMEM((tall, wide), jnp.bfloat16),
                pltpu.VMEM((wide, width), jnp.float32),
                pltpu.VMEM((rows, width), jnp.float32),
                pltpu.VMEM((across, rows // 2, width + 128), jnp.int32),
                pltpu.VMEM((along, rows // 2, width + 128), jnp.int32),
                pltpu.VMEM((across, rows // 2, width + 128), jnp.int32),
                pltpu.VMEM((along, rows // 2, width + 128), jnp.int32),
                pltpu.VMEM((across, rows, width), jnp.float32),
                pltpu.VMEM((across, 16, TILE), jnp.float32),
                pltpu.VMEM((along, 16, TILE), jnp.float32),
                dma((across,)),
                dma((across,)),
            ] + [dma((across,)), dma((across,)), dma((along,)), dma((along,))] * 3,
            compiler_params=pltpu.CompilerParams(
                collective_id=0, has_side_effects=True, vmem_limit_bytes=48 * 2**20),
        )(tile_mask, jnp.concatenate([images, texts], axis=0))
        return image_grads, text_grads, loss[0, 0]

    return jax.shard_map(
        on_device,
        mesh=mesh,
        in_specs=(P(("blk", "grp"), None), P(("blk", "grp"), None), P()),
        out_specs=(P(("blk", "grp"), None), P(("blk", "grp"), None), P()),
        check_vma=False,
    )
```

```python
import functools

import jax
import jax.numpy as jnp
from jax import lax
from jax.experimental import pallas as pl
from jax.experimental.pallas import tpu as pltpu
from jax.sharding import PartitionSpec as P

TILE = 128
TEMP = 10.0
BIAS = -2.0
EPS = 1e-06
LOG_2 = 0.6931471805599453
MESH = pl.DeviceIdType.MESH


def split_of(groups, loops, rows):
    best = None
    for inner in range(1, loops + 1):
        if loops % inner or (groups * inner * rows) % TILE:
            continue
        cost = groups * inner + loops // inner
        if best is None or cost <= best[0]:
            best = (cost, inner)
    return best[1]


def inverse_norm(x):
    return lax.rsqrt(jnp.sum(x * x, axis=-1, keepdims=True) + EPS)


def backward(x, g):
    r = inverse_norm(x)
    u = x * r
    return r * (g - u * jnp.sum(u * g, axis=-1, keepdims=True))


def flipped(place, bits):
    bit = 1
    while bit <= bits:
        if bits & bit:
            place = place + bit - 2 * bit * ((place // bit) % 2)
        bit *= 2
    return place


def step_of(exponent):
    return jnp.exp((exponent - 15.0) * LOG_2)


def pack(value):
    half = value.shape[0] // 2
    most = jnp.max(jnp.abs(value), axis=-1, keepdims=True)
    exponent = jnp.floor(jnp.log(jnp.maximum(most, 1e-30)) * (1.0 / LOG_2)) + 1.0
    fixed = jnp.clip(jnp.round(value * (1.0 / step_of(exponent))), -32767.0, 32767.0)
    fixed = jnp.concatenate(
        [fixed, jnp.broadcast_to(exponent, (value.shape[0], 128))], axis=1).astype(jnp.int32)
    return fixed[:half] * 65536 + (fixed[half:] & 65535)


def unpack(words):
    low = lax.shift_right_arithmetic(lax.shift_left(words, 16), 16)
    fixed = jnp.concatenate([lax.shift_right_arithmetic(words, 16), low], axis=0).astype(jnp.float32)
    width = fixed.shape[1] - 128
    return fixed[:, :width] * step_of(fixed[:, width:width + 1])


def kernel(groups, loops, inner, mask_hbm, img_hbm, txt_hbm,
           img_out, txt_out, loss_out,
           mask_s, mask_v, img_ref, txt_ref,
           imgs, imgs_t, txts, coef, img_part, txt_part, img_go, txt_go, img_in, txt_in, sib_in,
           img_res, txt_res, loss_a, loss_b,
           load_sem, sib_send, sib_recv,
           img_send, img_recv, txt_send, txt_recv,
           ip_send, ip_recv, tp_send, tp_recv,
           la_send, la_recv, lb_send, lb_recv):
    rows = img_ref.shape[0]
    across = groups * inner
    along = loops // inner
    g = lax.axis_index("grp")
    b = lax.axis_index("blk")
    o, i = b // inner, b % inner
    m = i * groups + g
    wide, tall = across * rows, along * rows
    core = groups

    def image_peer(d):
        p = flipped(m, d)
        return p, {"grp": p % groups, "blk": o * inner + p // groups}

    def text_peer(d):
        p = flipped(o, d)
        return p, {"grp": g, "blk": p * inner + i}

    def block(ref, p):
        return ref.at[pl.ds(pl.multiple_of(p * rows, rows), rows)]

    def copy(src, dst, send, recv, to):
        return pltpu.make_async_remote_copy(
            src_ref=src, dst_ref=dst, send_sem=send, recv_sem=recv,
            device_id=to, device_id_type=MESH)

    near = [d for d in range(1, across) if not d & core]

    def image_copy(d):
        return copy(block(imgs, m), block(imgs, m), img_send.at[d], img_recv.at[m], image_peer(d)[1])

    def image_relay(d):
        p = flipped(m, d)
        return copy(block(imgs, p), block(imgs, p), img_send.at[d + core], img_recv.at[p],
                    image_peer(core)[1])

    def image_arrival(d):
        p = flipped(m, d)
        return copy(block(imgs, p), block(imgs, p), img_send.at[d], img_recv.at[p], image_peer(d)[1])

    even = [d for d in range(1, along) if not d & 1]

    def text_copy(d):
        return copy(block(txts, o), block(txts, o), txt_send.at[d], txt_recv.at[o], text_peer(d)[1])

    def text_relay(d):
        p = flipped(o, d)
        return copy(block(txts, p), block(txts, p), txt_send.at[d + 1], txt_recv.at[p],
                    text_peer(1)[1])

    def text_arrival(d):
        p = flipped(o, d)
        return copy(block(txts, p), block(txts, p), txt_send.at[d], txt_recv.at[p], text_peer(d)[1])

    def sibling_copy(d, arriving=False):
        p = flipped(m, d if arriving else d + core)
        return copy(block(img_part, p), sib_in.at[d], sib_send.at[d], sib_recv.at[d],
                    image_peer(core)[1])

    def image_sum_copy(d, arriving=False):
        p, to = image_peer(d)
        at = p if arriving else m
        return copy(img_go.at[p], img_in.at[at], ip_send.at[d], ip_recv.at[at], to)

    def text_sum_copy(d, arriving=False):
        p, to = text_peer(d)
        at = p if arriving else o
        return copy(txt_go.at[p], txt_in.at[at], tp_send.at[d], tp_recv.at[at], to)

    def loss_a_copy(d, arriving=False):
        p, to = image_peer(d)
        at = p if arriving else m
        return copy(loss_a.at[m], loss_a.at[at], la_send.at[d], la_recv.at[at], to)

    def loss_b_copy(d, arriving=False):
        p, to = text_peer(d)
        at = p if arriving else o
        return copy(loss_b.at[o], loss_b.at[at], lb_send.at[d], lb_recv.at[at], to)

    loads = [pltpu.make_async_copy(src, dst, load_sem.at[k]) for k, (src, dst) in enumerate(
        [(txt_hbm, txt_ref), (img_hbm, img_ref), (mask_hbm, mask_s), (mask_hbm, mask_v)])]
    for load in loads:
        load.start()
    barrier = pltpu.get_barrier_semaphore()
    for d in range(1, along):
        pl.semaphore_signal(barrier, inc=1, device_id=text_peer(d)[1], device_id_type=MESH)
    for d in range(1, across):
        pl.semaphore_signal(barrier, inc=1, device_id=image_peer(d)[1], device_id_type=MESH)

    loads[0].wait()
    x = txt_ref[...].astype(jnp.float32)
    block(txts, o)[...] = (x * inverse_norm(x)).astype(jnp.bfloat16)
    loads[1].wait()
    x = img_ref[...].astype(jnp.float32)
    block(imgs, m)[...] = (x * inverse_norm(x)).astype(jnp.bfloat16)
    pl.semaphore_wait(barrier, along + across - 2)

    for d in even[::-1] + [1] * (along > 1):
        text_copy(d).start()
    for d in near[::-1] + [core]:
        image_copy(d).start()
    loads[2].wait()
    loads[3].wait()
    for d in near[:1]:
        image_arrival(d).wait_recv()
        image_relay(d).start()
    for d in even:
        text_arrival(d).wait_recv()
        text_relay(d).start()
    for d in near[1:]:
        image_arrival(d).wait_recv()
        image_relay(d).start()
    for d in [core] + [d + core for d in near]:
        image_arrival(d).wait_recv()

    imgs_t[...] = imgs[...].T
    ready = [0] + even
    late = [d + 1 for d in ready if d + 1 < along]
    batches = [part[k:k + 4] for part in (ready, late) for k in range(0, len(part), 4)]
    iota = lax.broadcasted_iota(jnp.int32, (rows, wide), 0)
    image_ids = o * wide + lax.broadcasted_iota(jnp.int32, (rows, wide), 1)
    loss = jnp.zeros((rows, TILE), jnp.float32)

    def send_text_sums(batch, value):
        sums = jnp.dot(value, imgs[...], preferred_element_type=jnp.float32)
        for k, d in enumerate(batch):
            part = sums[k * rows:(k + 1) * rows]
            if d:
                txt_go[flipped(o, d)] = pack(part)
                text_sum_copy(d).start()
            else:
                txt_part[...] = part

    for batch in batches:
        places = [flipped(o, d) for d in batch]
        for d in batch:
            if d & 1:
                text_arrival(d).wait_recv()
        logits = TEMP * jnp.dot(
            jnp.concatenate([block(txts, p)[...] for p in places], axis=0), imgs_t[...],
            preferred_element_type=jnp.float32) + BIAS
        held, matched = [], []
        for p in places:
            start = ((p * inner + i) * groups + g) * rows
            held.append(jnp.concatenate([
                jnp.full((rows, TILE), mask_s[start // TILE, (o * wide) // TILE + j], jnp.int32)
                for j in range(wide // TILE)], axis=1))
            matched.append((start + iota == image_ids).astype(jnp.int32))
        matched = jnp.concatenate(matched, axis=0) != 0
        valid = (jnp.concatenate(held, axis=0) == 0) | matched
        z = jnp.where(matched, -logits, logits)
        e = jnp.exp(-jnp.abs(logits))
        terms = jnp.where(valid, jnp.maximum(z, 0.0) + jnp.log1p(e), 0.0)
        loss += sum(terms[k * rows:(k + 1) * rows, j * TILE:(j + 1) * TILE]
                    for k in range(len(batch)) for j in range(wide // TILE))
        sig = jnp.where(logits >= 0, 1.0, e) / (1.0 + e)
        value = jnp.where(valid, sig - matched.astype(jnp.float32), 0.0).astype(jnp.bfloat16)
        for k, p in enumerate(places):
            block(coef, p)[...] = value[k * rows:(k + 1) * rows]
        if batch is not batches[-1]:
            send_text_sums(batch, value)
    loss_a[m] = jnp.sum(loss.reshape(rows // 8, 8, TILE), axis=0)
    half = across // 2
    for far in (1, 0):
        at = flipped(m, far * half) // half * half * rows
        at = pl.multiple_of(at, half * rows)
        img_part[pl.ds(at, half * rows)] = lax.dot_general(
            coef[:, pl.ds(at, half * rows)], txts[...], (((0,), (0,)), ((), ())),
            preferred_element_type=jnp.float32)
        for d in near[::-1] + [0]:
            if (d >= half) == bool(far):
                sibling_copy(d).start()
    send_text_sums(batches[-1], value)
    for d in range(1, across):
        loss_a_copy(d).start()
    for d in near[::-1]:
        p = flipped(m, d)
        sibling_copy(d, True).wait_recv()
        img_go[p] = pack(block(img_part, p)[...] + sib_in[d])
        image_sum_copy(d).start()

    for d in range(1, across):
        loss_a_copy(d, True).wait_recv()
    loss_b[o] = jnp.sum(loss_a[...], axis=0)
    for d in range(1, along):
        loss_b_copy(d).start()

    total = txt_part[...]
    for d in range(1, along):
        text_sum_copy(d, True).wait_recv()
        total += unpack(txt_in[flipped(o, d)])
    txt_res[...] = backward(txt_ref[...].astype(jnp.float32), TEMP * total)
    txt_store = pltpu.make_async_copy(txt_res, txt_out, load_sem.at[0])
    txt_store.start()

    sibling_copy(0, True).wait_recv()
    total = block(img_part, m)[...] + sib_in[0]
    for d in near[::-1]:
        image_sum_copy(d, True).wait_recv()
        total += unpack(img_in[flipped(m, d)])
    img_res[...] = backward(img_ref[...].astype(jnp.float32), TEMP * total)
    img_store = pltpu.make_async_copy(img_res, img_out, load_sem.at[1])
    img_store.start()

    for d in range(1, along):
        loss_b_copy(d, True).wait_recv()
    loss = jnp.sum(jnp.sum(loss_b[...], axis=0), keepdims=True)
    open_tiles = jnp.sum((mask_v[...] == 0).astype(jnp.float32), keepdims=True)
    loss_out[...] = loss / (open_tiles * (TILE * TILE) + (loops * groups * rows))

    for d in near:
        image_relay(d).wait_send()
        image_sum_copy(d).wait_send()
    for d in near + [core]:
        image_copy(d).wait_send()
    for d in near + [0]:
        sibling_copy(d).wait_send()
    for d in range(1, across):
        loss_a_copy(d).wait_send()
    for d in even:
        text_relay(d).wait_send()
    for d in even + [1] * (along > 1):
        text_copy(d).wait_send()
    for d in range(1, along):
        text_sum_copy(d).wait_send()
        loss_b_copy(d).wait_send()
    txt_store.wait()
    img_store.wait()


def solution(mesh):
    groups, loops = mesh.shape["grp"], mesh.shape["blk"]

    def on_device(images, texts, tile_mask):
        rows, width = images.shape
        inner = split_of(groups, loops, rows)
        across, along = groups * inner, loops // inner
        wide, tall = across * rows, along * rows
        dma = pltpu.SemaphoreType.DMA
        vmem = pl.BlockSpec(memory_space=pltpu.VMEM)
        hbm = pl.BlockSpec(memory_space=pltpu.HBM)
        image_grads, text_grads, loss = pl.pallas_call(
            functools.partial(kernel, groups, loops, inner),
            out_shape=(
                jax.ShapeDtypeStruct((rows, width), jnp.float32),
                jax.ShapeDtypeStruct((rows, width), jnp.float32),
                jax.ShapeDtypeStruct((1, 1), jnp.float32),
            ),
            in_specs=[hbm] * 3,
            out_specs=(hbm, hbm, vmem),
            scratch_shapes=[
                pltpu.SMEM(tile_mask.shape, jnp.int32),
                pltpu.VMEM(tile_mask.shape, jnp.int32),
                pltpu.VMEM((rows, width), jnp.bfloat16),
                pltpu.VMEM((rows, width), jnp.bfloat16),
                pltpu.VMEM((wide, width), jnp.bfloat16),
                pltpu.VMEM((width, wide), jnp.bfloat16),
                pltpu.VMEM((tall, width), jnp.bfloat16),
                pltpu.VMEM((tall, wide), jnp.bfloat16),
                pltpu.VMEM((wide, width), jnp.float32),
                pltpu.VMEM((rows, width), jnp.float32),
                pltpu.VMEM((across, rows // 2, width + 128), jnp.int32),
                pltpu.VMEM((along, rows // 2, width + 128), jnp.int32),
                pltpu.VMEM((across, rows // 2, width + 128), jnp.int32),
                pltpu.VMEM((along, rows // 2, width + 128), jnp.int32),
                pltpu.VMEM((across, rows, width), jnp.float32),
                pltpu.VMEM((rows, width), jnp.float32),
                pltpu.VMEM((rows, width), jnp.float32),
                pltpu.VMEM((across, 8, TILE), jnp.float32),
                pltpu.VMEM((along, 8, TILE), jnp.float32),
                dma((4,)),
                dma((across,)),
                dma((across,)),
            ] + [dma((across,)), dma((across,)), dma((along,)), dma((along,))] * 3,
            compiler_params=pltpu.CompilerParams(
                collective_id=0, has_side_effects=True, vmem_limit_bytes=63_192_064),
        )(tile_mask, images, texts)
        return image_grads, text_grads, loss[0, 0]

    return jax.shard_map(
        on_device,
        mesh=mesh,
        in_specs=(P(("blk", "grp"), None), P(("blk", "grp"), None), P()),
        out_specs=(P(("blk", "grp"), None), P(("blk", "grp"), None), P()),
        check_vma=False,
    )
```

```python
import functools

import jax
import jax.numpy as jnp
from jax import lax
from jax.experimental import pallas as pl
from jax.experimental.pallas import tpu as pltpu
from jax.sharding import PartitionSpec as P

TILE = 128
TEMP = 10.0
BIAS = -2.0
EPS = 1e-06
LOG_2 = 0.6931471805599453
MESH = pl.DeviceIdType.MESH


def split_of(groups, loops, rows):
    best = None
    for inner in range(1, loops + 1):
        if loops % inner or (groups * inner * rows) % TILE:
            continue
        cost = groups * inner + loops // inner
        if best is None or cost <= best[0]:
            best = (cost, inner)
    return best[1]


def inverse_norm(x):
    return lax.rsqrt(jnp.sum(x * x, axis=-1, keepdims=True) + EPS)


def backward(x, g):
    r = inverse_norm(x)
    u = x * r
    return r * (g - u * jnp.sum(u * g, axis=-1, keepdims=True))


def flipped(place, bits):
    bit = 1
    while bit <= bits:
        if bits & bit:
            place = place + bit - 2 * bit * ((place // bit) % 2)
        bit *= 2
    return place


def step_of(exponent):
    return jnp.exp((exponent - 15.0) * LOG_2)


def pack(value):
    half = value.shape[0] // 2
    most = jnp.max(jnp.abs(value), axis=-1, keepdims=True)
    exponent = jnp.floor(jnp.log(jnp.maximum(most, 1e-30)) * (1.0 / LOG_2)) + 1.0
    fixed = jnp.clip(jnp.round(value * (1.0 / step_of(exponent))), -32767.0, 32767.0)
    fixed = jnp.concatenate(
        [fixed, jnp.broadcast_to(exponent, (value.shape[0], 128))], axis=1).astype(jnp.int32)
    return fixed[:half] * 65536 + (fixed[half:] & 65535)


def unpack(words):
    low = lax.shift_right_arithmetic(lax.shift_left(words, 16), 16)
    fixed = jnp.concatenate([lax.shift_right_arithmetic(words, 16), low], axis=0).astype(jnp.float32)
    width = fixed.shape[1] - 128
    return fixed[:, :width] * step_of(fixed[:, width:width + 1])


def kernel(groups, loops, inner, mask_hbm, img_hbm, txt_hbm,
           img_out, txt_out, loss_out,
           mask_s, mask_v, img_ref, txt_ref,
           imgs, imgs_t, txts, coef, img_part, txt_part, img_go, txt_go, img_in, txt_in, sib_in,
           img_res, txt_res, loss_a, loss_b,
           load_sem, sib_send, sib_recv,
           img_send, img_recv, txt_send, txt_recv,
           ip_send, ip_recv, tp_send, tp_recv,
           la_send, la_recv, lb_send, lb_recv):
    rows = img_ref.shape[0]
    across = groups * inner
    along = loops // inner
    g = lax.axis_index("grp")
    b = lax.axis_index("blk")
    o, i = b // inner, b % inner
    m = i * groups + g
    wide, tall = across * rows, along * rows
    core = groups

    def image_peer(d):
        p = flipped(m, d)
        return p, {"grp": p % groups, "blk": o * inner + p // groups}

    def text_peer(d):
        p = flipped(o, d)
        return p, {"grp": g, "blk": p * inner + i}

    def block(ref, p):
        return ref.at[pl.ds(pl.multiple_of(p * rows, rows), rows)]

    def copy(src, dst, send, recv, to):
        return pltpu.make_async_remote_copy(
            src_ref=src, dst_ref=dst, send_sem=send, recv_sem=recv,
            device_id=to, device_id_type=MESH)

    near = [d for d in range(1, across) if not d & core]

    def image_copy(d):
        return copy(block(imgs, m), block(imgs, m), img_send.at[d], img_recv.at[m], image_peer(d)[1])

    def image_relay(d):
        p = flipped(m, d)
        return copy(block(imgs, p), block(imgs, p), img_send.at[d + core], img_recv.at[p],
                    image_peer(core)[1])

    def image_arrival(d):
        p = flipped(m, d)
        return copy(block(imgs, p), block(imgs, p), img_send.at[d], img_recv.at[p], image_peer(d)[1])

    even = [d for d in range(1, along) if not d & 1]

    def text_copy(d):
        return copy(block(txts, o), block(txts, o), txt_send.at[d], txt_recv.at[o], text_peer(d)[1])

    def text_relay(d):
        p = flipped(o, d)
        return copy(block(txts, p), block(txts, p), txt_send.at[d + 1], txt_recv.at[p],
                    text_peer(1)[1])

    def text_arrival(d):
        p = flipped(o, d)
        return copy(block(txts, p), block(txts, p), txt_send.at[d], txt_recv.at[p], text_peer(d)[1])

    def sibling_copy(d, arriving=False):
        p = flipped(m, d if arriving else d + core)
        return copy(block(img_part, p), sib_in.at[d], sib_send.at[d], sib_recv.at[d],
                    image_peer(core)[1])

    def image_sum_copy(d, arriving=False):
        p, to = image_peer(d)
        at = p if arriving else m
        return copy(img_go.at[p], img_in.at[at], ip_send.at[d], ip_recv.at[at], to)

    def text_sum_copy(d, arriving=False):
        p, to = text_peer(d)
        at = p if arriving else o
        return copy(txt_go.at[p], txt_in.at[at], tp_send.at[d], tp_recv.at[at], to)

    def loss_a_copy(d, arriving=False):
        p, to = image_peer(d)
        at = p if arriving else m
        return copy(loss_a.at[m], loss_a.at[at], la_send.at[d], la_recv.at[at], to)

    def loss_b_copy(d, arriving=False):
        p, to = text_peer(d)
        at = p if arriving else o
        return copy(loss_b.at[o], loss_b.at[at], lb_send.at[d], lb_recv.at[at], to)

    loads = [pltpu.make_async_copy(src, dst, load_sem.at[k]) for k, (src, dst) in enumerate(
        [(txt_hbm, txt_ref), (img_hbm, img_ref), (mask_hbm, mask_s), (mask_hbm, mask_v)])]
    for load in loads:
        load.start()
    barrier = pltpu.get_barrier_semaphore()
    for d in range(1, along):
        pl.semaphore_signal(barrier, inc=1, device_id=text_peer(d)[1], device_id_type=MESH)
    for d in range(1, across):
        pl.semaphore_signal(barrier, inc=1, device_id=image_peer(d)[1], device_id_type=MESH)

    loads[0].wait()
    x = txt_ref[...].astype(jnp.float32)
    block(txts, o)[...] = (x * inverse_norm(x)).astype(jnp.bfloat16)
    loads[1].wait()
    x = img_ref[...].astype(jnp.float32)
    block(imgs, m)[...] = (x * inverse_norm(x)).astype(jnp.bfloat16)
    pl.semaphore_wait(barrier, along + across - 2)

    for d in even[::-1] + [1] * (along > 1):
        text_copy(d).start()
    for d in near[::-1] + [core]:
        image_copy(d).start()
    loads[2].wait()
    loads[3].wait()
    for d in near:
        image_arrival(d).wait_recv()
        image_relay(d).start()
    for d in even:
        text_arrival(d).wait_recv()
        text_relay(d).start()
    for d in [core] + [d + core for d in near]:
        image_arrival(d).wait_recv()

    imgs_t[...] = imgs[...].T
    ready = [0] + even
    late = [d + 1 for d in ready if d + 1 < along]
    batches = [part[k:k + 4] for part in (ready, late) for k in range(0, len(part), 4)]
    iota = lax.broadcasted_iota(jnp.int32, (rows, wide), 0)
    image_ids = o * wide + lax.broadcasted_iota(jnp.int32, (rows, wide), 1)
    loss = jnp.zeros((rows, TILE), jnp.float32)

    def send_text_sums(batch, value):
        sums = jnp.dot(value, imgs[...], preferred_element_type=jnp.float32)
        for k, d in enumerate(batch):
            part = sums[k * rows:(k + 1) * rows]
            if d:
                txt_go[flipped(o, d)] = pack(part)
                text_sum_copy(d).start()
            else:
                txt_part[...] = part

    for batch in batches:
        places = [flipped(o, d) for d in batch]
        for d in batch:
            if d & 1:
                text_arrival(d).wait_recv()
        logits = TEMP * jnp.dot(
            jnp.concatenate([block(txts, p)[...] for p in places], axis=0), imgs_t[...],
            preferred_element_type=jnp.float32) + BIAS
        held, matched = [], []
        for p in places:
            start = ((p * inner + i) * groups + g) * rows
            held.append(jnp.concatenate([
                jnp.full((rows, TILE), mask_s[start // TILE, (o * wide) // TILE + j], jnp.int32)
                for j in range(wide // TILE)], axis=1))
            matched.append((start + iota == image_ids).astype(jnp.int32))
        matched = jnp.concatenate(matched, axis=0) != 0
        valid = (jnp.concatenate(held, axis=0) == 0) | matched
        z = jnp.where(matched, -logits, logits)
        e = jnp.exp(-jnp.abs(logits))
        terms = jnp.where(valid, jnp.maximum(z, 0.0) + jnp.log1p(e), 0.0)
        loss += sum(terms[k * rows:(k + 1) * rows, j * TILE:(j + 1) * TILE]
                    for k in range(len(batch)) for j in range(wide // TILE))
        sig = jnp.where(logits >= 0, 1.0, e) / (1.0 + e)
        value = jnp.where(valid, sig - matched.astype(jnp.float32), 0.0).astype(jnp.bfloat16)
        for k, p in enumerate(places):
            block(coef, p)[...] = value[k * rows:(k + 1) * rows]
        if batch is not batches[-1]:
            send_text_sums(batch, value)
    loss_a[m] = jnp.sum(loss.reshape(rows // 8, 8, TILE), axis=0)
    half = across // 2
    for far in (1, 0):
        at = flipped(m, far * half) // half * half * rows
        at = pl.multiple_of(at, half * rows)
        img_part[pl.ds(at, half * rows)] = lax.dot_general(
            coef[:, pl.ds(at, half * rows)], txts[...], (((0,), (0,)), ((), ())),
            preferred_element_type=jnp.float32)
        for d in near[::-1] + [0]:
            if (d >= half) == bool(far):
                sibling_copy(d).start()
    send_text_sums(batches[-1], value)
    for d in range(1, across):
        loss_a_copy(d).start()
    for d in near[::-1]:
        p = flipped(m, d)
        sibling_copy(d, True).wait_recv()
        img_go[p] = pack(block(img_part, p)[...] + sib_in[d])
        image_sum_copy(d).start()

    for d in range(1, across):
        loss_a_copy(d, True).wait_recv()
    loss_b[o] = jnp.sum(loss_a[...], axis=0)
    for d in range(1, along):
        loss_b_copy(d).start()

    total = txt_part[...]
    for d in range(1, along):
        text_sum_copy(d, True).wait_recv()
        total += unpack(txt_in[flipped(o, d)])
    txt_res[...] = backward(txt_ref[...].astype(jnp.float32), TEMP * total)
    txt_store = pltpu.make_async_copy(txt_res, txt_out, load_sem.at[0])
    txt_store.start()

    sibling_copy(0, True).wait_recv()
    total = block(img_part, m)[...] + sib_in[0]
    for d in near[::-1]:
        image_sum_copy(d, True).wait_recv()
        total += unpack(img_in[flipped(m, d)])
    img_res[...] = backward(img_ref[...].astype(jnp.float32), TEMP * total)
    img_store = pltpu.make_async_copy(img_res, img_out, load_sem.at[1])
    img_store.start()

    for d in range(1, along):
        loss_b_copy(d, True).wait_recv()
    loss = jnp.sum(jnp.sum(loss_b[...], axis=0), keepdims=True)
    open_tiles = jnp.sum((mask_v[...] == 0).astype(jnp.float32), keepdims=True)
    loss_out[...] = loss / (open_tiles * (TILE * TILE) + (loops * groups * rows))

    for d in near:
        image_relay(d).wait_send()
        image_sum_copy(d).wait_send()
    for d in near + [core]:
        image_copy(d).wait_send()
    for d in near + [0]:
        sibling_copy(d).wait_send()
    for d in range(1, across):
        loss_a_copy(d).wait_send()
    for d in even:
        text_relay(d).wait_send()
    for d in even + [1] * (along > 1):
        text_copy(d).wait_send()
    for d in range(1, along):
        text_sum_copy(d).wait_send()
        loss_b_copy(d).wait_send()
    txt_store.wait()
    img_store.wait()


def solution(mesh):
    groups, loops = mesh.shape["grp"], mesh.shape["blk"]

    def on_device(images, texts, tile_mask):
        rows, width = images.shape
        inner = split_of(groups, loops, rows)
        across, along = groups * inner, loops // inner
        wide, tall = across * rows, along * rows
        dma = pltpu.SemaphoreType.DMA
        vmem = pl.BlockSpec(memory_space=pltpu.VMEM)
        hbm = pl.BlockSpec(memory_space=pltpu.HBM)
        image_grads, text_grads, loss = pl.pallas_call(
            functools.partial(kernel, groups, loops, inner),
            out_shape=(
                jax.ShapeDtypeStruct((rows, width), jnp.float32),
                jax.ShapeDtypeStruct((rows, width), jnp.float32),
                jax.ShapeDtypeStruct((1, 1), jnp.float32),
            ),
            in_specs=[hbm] * 3,
            out_specs=(hbm, hbm, vmem),
            scratch_shapes=[
                pltpu.SMEM(tile_mask.shape, jnp.int32),
                pltpu.VMEM(tile_mask.shape, jnp.int32),
                pltpu.VMEM((rows, width), jnp.bfloat16),
                pltpu.VMEM((rows, width), jnp.bfloat16),
                pltpu.VMEM((wide, width), jnp.bfloat16),
                pltpu.VMEM((width, wide), jnp.bfloat16),
                pltpu.VMEM((tall, width), jnp.bfloat16),
                pltpu.VMEM((tall, wide), jnp.bfloat16),
                pltpu.VMEM((wide, width), jnp.float32),
                pltpu.VMEM((rows, width), jnp.float32),
                pltpu.VMEM((across, rows // 2, width + 128), jnp.int32),
                pltpu.VMEM((along, rows // 2, width + 128), jnp.int32),
                pltpu.VMEM((across, rows // 2, width + 128), jnp.int32),
                pltpu.VMEM((along, rows // 2, width + 128), jnp.int32),
                pltpu.VMEM((across, rows, width), jnp.float32),
                pltpu.VMEM((rows, width), jnp.float32),
                pltpu.VMEM((rows, width), jnp.float32),
                pltpu.VMEM((across, 8, TILE), jnp.float32),
                pltpu.VMEM((along, 8, TILE), jnp.float32),
                dma((4,)),
                dma((across,)),
                dma((across,)),
            ] + [dma((across,)), dma((across,)), dma((along,)), dma((along,))] * 3,
            compiler_params=pltpu.CompilerParams(
                collective_id=0, has_side_effects=True, vmem_limit_bytes=62_900_000),
        )(tile_mask, images, texts)
        return image_grads, text_grads, loss[0, 0]

    return jax.shard_map(
        on_device,
        mesh=mesh,
        in_specs=(P(("blk", "grp"), None), P(("blk", "grp"), None), P()),
        out_specs=(P(("blk", "grp"), None), P(("blk", "grp"), None), P()),
        check_vma=False,
    )
```
